256 devices in a mesh: row: 16 (over z, core), col: 16 (over y, x).
Axes of the slice: x: 4, y: 4, z: 8, core: 2. Of those that a mesh axis runs over, the one named last changes fastest.
Arguments:
- affinity: float32 [16384, 16384], P('row', 'col'), as said below
Outputs:
- reduced: float32 [16384, 16384], P('row', 'col')
Inputs may be any that keep to these rules, and one draw needn't show every extreme that they name: The matrix that affinity stores is exactly symmetric in global indexing.
All inputs are finite; a program needn't handle non-finite values.
Results may differ from the reference program's by a relative error of at most 0.0003.
Values sent between devices are 32-bit elements; how exact they have to be, the bound alone decides.
A program may use at most 64 MiB of HBM per device.

```python
import math
import jax
import jax.numpy as jnp
from jax import lax

N = 16384
B = 256
PANELS = 2
NS_STEPS = 12
ROW_BLOCKS = 4
COL_BLOCKS = 4
N_ROW = 16
N_COL = 16


def draw_affinity(key, part):
    noise_key = jax.random.fold_in(key, 11)
    scale_key = jax.random.fold_in(key, 12)
    uniform_noise = jax.random.uniform(noise_key, (N, N), jnp.float32, -1.0, 1.0)
    sym_part = 0.5 * (uniform_noise + uniform_noise.T)
    scales = jnp.exp(jax.random.uniform(scale_key, (N,), jnp.float32, 0.0, math.log(10.0)))
    dense_matrix = 0.25 * sym_part * (scales[:, None] * scales[None, :])
    lower_index = jnp.arange(N - B, dtype=jnp.int32)
    upper_index = lower_index + B
    band_value = 64.0 * (scales[upper_index] * scales[lower_index])
    dense_matrix = dense_matrix.at[upper_index, lower_index].add(band_value)
    dense_matrix = dense_matrix.at[lower_index, upper_index].add(band_value)
    row_devices = N // (B * ROW_BLOCKS)
    col_devices = N // (B * COL_BLOCKS)
    rows_here = N // row_devices
    cols_here = N // col_devices
    stored_index = jnp.arange(N, dtype=jnp.int32)
    row_order = (stored_index % rows_here // B * row_devices + stored_index // rows_here) * B + stored_index % B
    col_order = (stored_index % cols_here // B * col_devices + stored_index // cols_here) * B + stored_index % B
    return jnp.take(jnp.take(dense_matrix, row_order, axis=0), col_order, axis=1)


def setup_inputs(seed: int = 0) -> dict:
    key_of = jax.random.split(jax.random.key(seed), 2)
    return {
        "affinity": draw_affinity(jax.random.fold_in(key_of[1], 71), 0),
    }


PRECISE = lax.Precision.HIGHEST

def matmul(first_op, second_op, first_dim, second_dim):
    return lax.dot_general(first_op.astype(jnp.float32), second_op.astype(jnp.float32), (((first_dim,), (second_dim,)), ((), ())), precision=PRECISE, preferred_element_type=jnp.float32)

def lower_inverse(square):
    lower_factor = jnp.linalg.cholesky(square)
    identity = jnp.eye(square.shape[0], dtype=jnp.float32)
    return lax.linalg.triangular_solve(lower_factor, identity, left_side=True, lower=True)

def reflector_parts(gram_matrix, top_block):
    inverse_low = lower_inverse(gram_matrix)
    top_basis = matmul(top_block, inverse_low, 1, 1)
    polar_part = top_basis
    for repeat in range(NS_STEPS):
        polar_part = 1.5 * polar_part - 0.5 * matmul(polar_part, matmul(polar_part, polar_part, 0, 0), 1, 0)
    cross_term = matmul(polar_part, top_basis, 0, 0)
    identity = jnp.eye(gram_matrix.shape[0], dtype=jnp.float32)
    metric = identity + cross_term + cross_term.T + matmul(polar_part, polar_part, 0, 0)
    metric_inv = lower_inverse(metric)
    middle = 2.0 * matmul(metric_inv, metric_inv, 0, 0)
    return (inverse_low, polar_part, middle)

def reference(affinity):
    rows_here = N // N_ROW
    cols_here = N // N_COL
    stored = jnp.arange(N, dtype=jnp.int32)
    row_blocks = stored % rows_here // B * N_ROW + stored // rows_here
    col_device = stored // cols_here
    col_global = stored % cols_here // B * N_COL + col_device
    col_within = stored % B
    row_place = (col_global % N_ROW * rows_here + col_global // N_ROW * B + col_within).astype(jnp.int32)
    matrix = affinity
    for panel_num in range(PANELS):
        col_start = panel_num % N_COL * cols_here + panel_num // N_COL * B
        panel_rows = jnp.where((row_blocks > panel_num)[:, None], matrix[:, col_start:col_start + B], 0.0)
        top_start = (panel_num + 1) % N_ROW * rows_here + (panel_num + 1) // N_ROW * B
        gram_matrix = matmul(panel_rows, panel_rows, 0, 0)
        inverse_low, polar_part, middle = reflector_parts(gram_matrix, panel_rows[top_start:top_start + B])
        reflect_rows = matmul(panel_rows, inverse_low, 1, 1).at[top_start:top_start + B].add(polar_part)
        reflect_cols = jnp.take(reflect_rows, row_place, axis=0)
        product_rows = matmul(matrix, reflect_cols, 1, 0)
        image_rows = matmul(product_rows, middle, 1, 0)
        coupling = matmul(reflect_rows, image_rows, 0, 0)
        shift_term = matmul(middle, coupling, 1, 0)
        companion_rows = image_rows - 0.5 * matmul(reflect_rows, shift_term, 1, 0)
        companion_cols = jnp.take(companion_rows, row_place, axis=0)
        matrix = matrix - matmul(jnp.concatenate((reflect_rows, companion_rows), 1), jnp.concatenate((companion_cols, reflect_cols), 1), 1, 1)
    return matrix
```

```python
import functools

import jax
import jax.numpy as jnp
from jax import lax
from jax.experimental import pallas as pl
from jax.experimental.pallas import tpu as pltpu
from jax.sharding import PartitionSpec as P

B = 256
PANELS = 2
NS_STEPS = 12
D = 16
PIECE = 64
SLICE = 16
MESH = pl.DeviceIdType.MESH
HIGHEST = lax.Precision.HIGHEST
VMEM_LIMIT = 56 * 1024 * 1024


def dot(first, second, first_dim, second_dim):
    return lax.dot_general(
        first,
        second,
        (((first_dim,), (second_dim,)), ((), ())),
        precision=HIGHEST,
        preferred_element_type=jnp.float32,
    )


def split(value):
    high = value.astype(jnp.bfloat16)
    return high, (value - high.astype(jnp.float32)).astype(jnp.bfloat16)


def dot_split(first, second, first_dim, second_dim):
    def one(x, y):
        return lax.dot_general(
            x, y, (((first_dim,), (second_dim,)), ((), ())), preferred_element_type=jnp.float32
        )

    return one(first[0], second[0]) + (one(first[0], second[1]) + one(first[1], second[0]))


def dot3(first, second, first_dim, second_dim):
    return dot_split(split(first), split(second), first_dim, second_dim)


def sublane(x, j):
    return jnp.broadcast_to(x[j : j + 1, :], x.shape)


def chol_inverse_128(d_ref):
    n = 128
    sub = lax.broadcasted_iota(jnp.int32, (8, n), 0)
    lane = lax.broadcasted_iota(jnp.int32, (8, n), 1)
    rows = [d_ref[8 * g : 8 * g + 8, :] for g in range(n // 8)]
    for g in range(n // 8):
        k0 = 8 * g
        own = (lane >= k0) & (lane < k0 + 8)
        unit = jnp.where(lane == sub + k0, 1.0, 0.0)
        cur = rows[g]
        cols = [jnp.broadcast_to(cur[:, k0 + j : k0 + j + 1], (8, n)) for j in range(8)]
        cur = jnp.where(own, unit, cur)
        recips, factors, pivots = [], {}, []
        diag = jnp.ones((8, n), jnp.float32)
        for j in range(8):
            d = sublane(cols[j], j)
            recips.append(1.0 / d)
            diag = jnp.where(sub == j, d, diag)
            f = jnp.where(sub > j, cols[j] * recips[j], 0.0)
            for l in range(j + 1, 8):
                factors[j, l] = sublane(cols[l], j)
                cols[l] = cols[l] - f * factors[j, l]
            pivots.append(sublane(cur, j))
            cur = cur - f * pivots[j]
        d_ref[k0 : k0 + 8, :] = jnp.where(lane < k0 + 8, cur, 0.0) / jnp.sqrt(diag)
        for i in range(g + 1, n // 8):
            low = rows[i]
            cols = [jnp.broadcast_to(low[:, k0 + j : k0 + j + 1], (8, n)) for j in range(8)]
            low = jnp.where(own, 0.0, low)
            for j in range(8):
                f = cols[j] * recips[j]
                for l in range(j + 1, 8):
                    cols[l] = cols[l] - f * factors[j, l]
                low = low - f * pivots[j]
            rows[i] = low


def chol_inverse(gram, out_ref, d_ref):
    half = B // 2
    d_ref[...] = gram[:half, :half]
    chol_inverse_128(d_ref)
    first = d_ref[...]
    below = dot(gram[half:, :half], first, 1, 1)
    d_ref[...] = gram[half:, half:] - dot(below, below, 1, 1)
    chol_inverse_128(d_ref)
    second = d_ref[...]
    out_ref[:half, :half] = first
    out_ref[:half, half:] = jnp.zeros((half, half), jnp.float32)
    out_ref[half:, :half] = -dot(second, dot(below, first, 1, 0), 1, 0)
    out_ref[half:, half:] = second


def eye():
    r = lax.broadcasted_iota(jnp.int32, (B, B), 0)
    c = lax.broadcasted_iota(jnp.int32, (B, B), 1)
    return jnp.where(r == c, 1.0, 0.0)


def factor_kernel(
    panel, a_ref, pr_ref, pq_ref, gt_ref,
    vr_ref, vq_ref, mid_ref, x_ref, kp_ref,
    inv_ref, d_ref, w_ref,
):
    p, q = lax.axis_index("row"), lax.axis_index("col")
    gt = gt_ref[...]
    gram = gt[:, :SLICE, :].reshape(B, B)
    block = gt[:, SLICE:, :].reshape(B, B)
    chol_inverse(gram, inv_ref, d_ref)
    inverse_low = inv_ref[...]
    top = dot(block, inverse_low, 1, 1)
    w_ref[...] = top

    def step(i, carry):
        w = w_ref[...]
        s = split(w)
        w_ref[...] = 1.5 * w - 0.5 * dot_split(s, split(dot_split(s, s, 0, 0)), 1, 0)
        return carry

    lax.fori_loop(0, NS_STEPS, step, 0)
    w = w_ref[...]
    cross = dot(w, top, 0, 0)
    metric = eye() + cross + cross.T + dot(w, w, 0, 0)
    guess = (40.0 / 41.0) * eye() - (8.0 / 41.0) * metric
    for i in range(4):
        mul = dot if i == 3 else dot3
        guess = guess + mul(guess, eye() - mul(metric, guess, 1, 0), 1, 0)
    mid_ref[...] = 2.0 * guess

    inv_split = split(inverse_low)
    for tile in range(4):
        rows = slice(tile * B, tile * B + B)
        vr_ref[rows, :] = dot_split(split(pr_ref[rows, :]), inv_split, 1, 1)
        vq_ref[rows, :] = dot_split(split(pq_ref[rows, :]), inv_split, 1, 1)
    here = jnp.where(p == panel + 1, 1.0, 0.0)
    vr_ref[:B, :] = vr_ref[:B, :] + here * w
    here = jnp.where(q == panel + 1, 1.0, 0.0)
    vq_ref[:B, :] = vq_ref[:B, :] + here * w

    vq = split(vq_ref[...])
    kp_ref[...] = jnp.zeros((B, B), jnp.float32)

    def tile_step(tile, carry):
        rows = pl.ds(pl.multiple_of(tile * B, B), B)
        x = dot_split(split(a_ref[rows, :]), vq, 1, 0)
        x_ref[rows, :] = x
        kp_ref[...] += dot3(vr_ref[rows, :], x, 0, 0)
        return carry

    lax.fori_loop(0, 4, tile_step, 0)


def factor(panel, matrix, pr, pq, gt):
    vmem = pl.BlockSpec(memory_space=pltpu.VMEM)
    tall = jax.ShapeDtypeStruct((4 * B, B), jnp.float32)
    square = jax.ShapeDtypeStruct((B, B), jnp.float32)
    return pl.pallas_call(
        functools.partial(factor_kernel, panel),
        out_shape=(tall, tall, square, tall, square),
        in_specs=[vmem] * 4,
        out_specs=(vmem,) * 5,
        scratch_shapes=[
            pltpu.VMEM((B, B), jnp.float32),
            pltpu.VMEM((B // 2, B // 2), jnp.float32),
            pltpu.VMEM((B, B), jnp.float32),
        ],
        compiler_params=pltpu.CompilerParams(vmem_limit_bytes=VMEM_LIMIT),
        name=f"factor_{panel}",
    )(matrix, pr, pq, gt)


def greet(p, q, partner):
    barrier = pltpu.get_barrier_semaphore()
    for i in range(1, D):
        pl.semaphore_signal(
            barrier, inc=1, device_id=(lax.rem(p + i, D), q), device_id_type=MESH
        )
        pl.semaphore_signal(
            barrier, inc=1, device_id=(p, lax.rem(q + i, D)), device_id_type=MESH
        )
    if partner:

        @pl.when(p != q)
        def _():
            pl.semaphore_signal(barrier, inc=1, device_id=(q, p), device_id_type=MESH)
            pl.semaphore_wait(barrier, 2 * (D - 1) + 1)

        @pl.when(p == q)
        def _():
            pl.semaphore_wait(barrier, 2 * (D - 1))

    else:
        pl.semaphore_wait(barrier, 2 * (D - 1))


def remote(src, dst, send, recv, target):
    return pltpu.make_async_remote_copy(
        src_ref=src, dst_ref=dst, send_sem=send, recv_sem=recv,
        device_id=target, device_id_type=MESH,
    )


def piece(index):
    return pl.ds(pl.multiple_of(index * PIECE, PIECE), PIECE)


def slab(index):
    return pl.ds(pl.multiple_of(index * SLICE, SLICE), SLICE)


def gather_col_start(ref, at, send, recv, p, q):
    for i in range(1, D):
        t = lax.rem(q + i, D)
        remote(ref.at[at(q)], ref.at[at(q)], send.at[i], recv.at[q], (p, t)).start()


def gather_col_wait(ref, at, send, recv, p, q):
    for i in range(1, D):
        t = lax.rem(q + i, D)
        remote(ref.at[at(t)], ref.at[at(t)], send.at[i], recv.at[t], (p, t)).wait_recv()


def gather_col_drain(ref, at, send, recv, p, q):
    for i in range(1, D):
        t = lax.rem(q + i, D)
        remote(ref.at[at(q)], ref.at[at(q)], send.at[i], recv.at[q], (p, t)).wait_send()


def gather_row_start(ref, send, recv, p, q):
    for i in range(0, D, 2):
        t = lax.rem(p + i, D) if i else p + 1 - 2 * lax.rem(p, 2)
        remote(ref.at[piece(p)], ref.at[piece(p)], send.at[i], recv.at[p], (t, q)).start()


def gather_row_pass(ref, send, recv, p, q):
    other = p + 1 - 2 * lax.rem(p, 2)
    for i in (2, 14, 4, 12, 6, 10, 8):
        t = lax.rem(p + i, D)
        remote(ref.at[piece(t)], ref.at[piece(t)], send.at[i], recv.at[t], (t, q)).wait_recv()
        remote(ref.at[piece(t)], ref.at[piece(t)], send.at[i + 1], recv.at[t], (other, q)).start()


def gather_row_wait(ref, send, recv, p, q):
    other = p + 1 - 2 * lax.rem(p, 2)
    for i in range(0, D, 2):
        t = lax.rem(other + i, D)
        remote(ref.at[piece(t)], ref.at[piece(t)], send.at[i], recv.at[t], (other, q)).wait_recv()


def gather_row_drain(ref, send, recv, p, q):
    other = p + 1 - 2 * lax.rem(p, 2)
    for i in range(0, D, 2):
        remote(ref.at[piece(p)], ref.at[piece(p)], send.at[i], recv.at[p], (other, q)).wait_send()
        if i:
            t = lax.rem(p + i, D)
            remote(
                ref.at[piece(t)], ref.at[piece(t)], send.at[i + 1], recv.at[t], (other, q)
            ).wait_send()


def panel_kernel(
    panel, a_ref, pr_ref, pq_ref, gt_ref,
    tall, wide, turned, gram, part, block,
    load, gram_s, gram_r, block_s, block_r, down_s, down_r, gt_s, gt_r,
    prs_s, prs_r, pr_s, pr_r, pqs_s, pqs_r, pq_s, pq_r,
):
    p, q = lax.axis_index("row"), lax.axis_index("col")
    greet(p, q, False)
    row_owner, col_owner = p == panel, q == panel
    whole = lambda index: index
    load_tall = pltpu.make_async_copy(a_ref.at[:, pl.ds(0, B)], tall, load.at[0])
    load_wide = pltpu.make_async_copy(a_ref.at[pl.ds(0, B), :], wide, load.at[1])

    @pl.when(col_owner)
    def _():
        load_tall.start()

    @pl.when(row_owner)
    def _():
        load_wide.start()
        load_wide.wait()

        @pl.when(q <= panel)
        def _():
            wide[:, :B] = jnp.zeros((B, B), jnp.float32)

        gram[...] = dot(wide[...], wide[...], 1, 1)
        for i in range(1, D):
            t = lax.rem(q + i, D)
            remote(gram.at[slab(t)], part.at[q], gram_s.at[i], gram_r.at[q], (p, t)).start()
        part[q] = gram[slab(q), :]

        @pl.when(q == panel + 1)
        def _():
            block[...] = wide[:, :B].T
            for i in range(1, D):
                t = lax.rem(q + i, D)
                remote(
                    block.at[slab(t)], gt_ref.at[t, pl.ds(SLICE, SLICE)],
                    block_s.at[i], block_r, (p, t),
                ).start()
            gt_ref[q, SLICE:, :] = block[slab(q), :]

        turned[...] = wide[...].T
        for i in range(1, D):
            t = lax.rem(p + i, D)
            remote(
                turned.at[piece(t)], pq_ref.at[piece(t)], pqs_s.at[i], pqs_r, (t, q)
            ).start()
        pq_ref[piece(p), :] = turned[piece(p), :]

    @pl.when(col_owner)
    def _():
        load_tall.wait()

        @pl.when(p <= panel)
        def _():
            tall[:B, :] = jnp.zeros((B, B), jnp.float32)

        for i in range(1, D):
            t = lax.rem(q + i, D)
            remote(tall.at[piece(t)], pr_ref.at[piece(t)], prs_s.at[i], prs_r, (p, t)).start()
        pr_ref[piece(q), :] = tall[piece(q), :]

    @pl.when(row_owner)
    def _():
        for i in range(1, D):
            t = lax.rem(q + i, D)
            remote(gram.at[slab(q)], part.at[t], gram_s.at[i], gram_r.at[t], (p, t)).wait_recv()
        total = part[0]
        for i in range(1, D):
            total = total + part[i]
        gt_ref[q, :SLICE, :] = total

        @pl.when(q != panel + 1)
        def _():
            remote(
                block.at[slab(q)], gt_ref.at[q, pl.ds(SLICE, SLICE)], block_s.at[0], block_r, (p, q)
            ).wait_recv()

        for i in range(1, D):
            t = lax.rem(p + i, D)
            remote(gt_ref.at[q], gt_ref.at[q], down_s.at[i], down_r, (t, q)).start()

    @pl.when(jnp.logical_not(row_owner))
    def _():
        remote(turned.at[piece(p)], pq_ref.at[piece(p)], pqs_s.at[0], pqs_r, (p, q)).wait_recv()

    gather_row_start(pq_ref, pq_s, pq_r, p, q)

    @pl.when(jnp.logical_not(col_owner))
    def _():
        remote(tall.at[piece(q)], pr_ref.at[piece(q)], prs_s.at[0], prs_r, (p, q)).wait_recv()

    gather_col_start(pr_ref, piece, pr_s, pr_r, p, q)

    @pl.when(jnp.logical_not(row_owner))
    def _():
        remote(gt_ref.at[q], gt_ref.at[q], down_s.at[0], down_r, (p, q)).wait_recv()

    gather_col_start(gt_ref, whole, gt_s, gt_r, p, q)
    gather_row_pass(pq_ref, pq_s, pq_r, p, q)
    gather_col_wait(pr_ref, piece, pr_s, pr_r, p, q)
    gather_col_wait(gt_ref, whole, gt_s, gt_r, p, q)
    gather_row_wait(pq_ref, pq_s, pq_r, p, q)
    gather_row_drain(pq_ref, pq_s, pq_r, p, q)
    gather_col_drain(pr_ref, piece, pr_s, pr_r, p, q)
    gather_col_drain(gt_ref, whole, gt_s, gt_r, p, q)

    @pl.when(row_owner)
    def _():
        for i in range(1, D):
            t = lax.rem(q + i, D)
            remote(gram.at[slab(t)], part.at[q], gram_s.at[i], gram_r.at[q], (p, t)).wait_send()
            t = lax.rem(p + i, D)
            remote(
                turned.at[piece(t)], pq_ref.at[piece(t)], pqs_s.at[i], pqs_r, (t, q)
            ).wait_send()
            remote(gt_ref.at[q], gt_ref.at[q], down_s.at[i], down_r, (t, q)).wait_send()

        @pl.when(q == panel + 1)
        def _():
            for i in range(1, D):
                t = lax.rem(q + i, D)
                remote(
                    block.at[slab(t)], gt_ref.at[t, pl.ds(SLICE, SLICE)],
                    block_s.at[i], block_r, (p, t),
                ).wait_send()

    @pl.when(col_owner)
    def _():
        for i in range(1, D):
            t = lax.rem(q + i, D)
            remote(tall.at[piece(t)], pr_ref.at[piece(t)], prs_s.at[i], prs_r, (p, t)).wait_send()


def share_panel(panel, matrix):
    vmem = pl.BlockSpec(memory_space=pltpu.VMEM)
    tall = jax.ShapeDtypeStruct((4 * B, B), jnp.float32)
    many, one = pltpu.SemaphoreType.DMA((D,)), pltpu.SemaphoreType.DMA
    return pl.pallas_call(
        functools.partial(panel_kernel, panel),
        out_shape=(tall, tall, jax.ShapeDtypeStruct((D, 2 * SLICE, B), jnp.float32)),
        in_specs=[pl.BlockSpec(memory_space=pl.ANY)],
        out_specs=(vmem,) * 3,
        scratch_shapes=[
            pltpu.VMEM((4 * B, B), jnp.float32),
            pltpu.VMEM((B, 4 * B), jnp.float32),
            pltpu.VMEM((4 * B, B), jnp.float32),
            pltpu.VMEM((B, B), jnp.float32),
            pltpu.VMEM((D, SLICE, B), jnp.float32),
            pltpu.VMEM((B, B), jnp.float32),
            pltpu.SemaphoreType.DMA((2,)),
            many, many, many, one, many, one, many, many,
            many, one, many, many, many, one, many, many,
        ],
        compiler_params=pltpu.CompilerParams(
            collective_id=1 + panel, has_side_effects=True, vmem_limit_bytes=VMEM_LIMIT
        ),
        name=f"share_panel_{panel}",
    )(matrix)


def image_kernel(
    x_ref, kp_ref, mid_ref, cp_ref, cq_ref, k_ref,
    parts, kparts, ksum, krows,
    x_s, x_r, kp_s, kp_r, kr_s, kr_r, k_s, k_r, cp_s, cp_r, turn_s, turn_r, cq_s, cq_r,
):
    p, q = lax.axis_index("row"), lax.axis_index("col")
    greet(p, q, True)
    for i in range(1, D):
        t = lax.rem(q + i, D)
        remote(kp_ref.at[slab(t)], kparts.at[q], kp_s.at[i], kp_r.at[q], (p, t)).start()
    for i in range(1, D):
        t = lax.rem(q + i, D)
        remote(x_ref.at[piece(t)], parts.at[q], x_s.at[i], x_r.at[q], (p, t)).start()
    kparts[q] = kp_ref[slab(q), :]
    parts[q] = x_ref[piece(q), :]

    for i in range(1, D):
        t = lax.rem(q + i, D)
        remote(kp_ref.at[slab(q)], kparts.at[t], kp_s.at[i], kp_r.at[t], (p, t)).wait_recv()
    total = kparts[0]
    for i in range(1, D):
        total = total + kparts[i]
    ksum[...] = total
    krows[p] = total
    for i in range(1, D):
        t = lax.rem(p + i, D)
        remote(ksum, krows.at[p], kr_s.at[i], kr_r.at[p], (t, q)).start()

    for i in range(1, D):
        t = lax.rem(q + i, D)
        remote(x_ref.at[piece(q)], parts.at[t], x_s.at[i], x_r.at[t], (p, t)).wait_recv()
    total = parts[0]
    for i in range(1, D):
        total = total + parts[i]
    image = dot(total, mid_ref[...], 1, 0)
    cp_ref[piece(q), :] = image

    @pl.when(p != q)
    def _():
        remote(cp_ref.at[piece(q)], cq_ref.at[piece(q)], turn_s, turn_r, (q, p)).start()

    @pl.when(p == q)
    def _():
        cq_ref[piece(p), :] = image

    gather_col_start(cp_ref, piece, cp_s, cp_r, p, q)

    for i in range(1, D):
        t = lax.rem(p + i, D)
        remote(ksum, krows.at[t], kr_s.at[i], kr_r.at[t], (t, q)).wait_recv()
    total = krows[0]
    for i in range(1, D):
        total = total + krows[i]
    k_ref[slab(q), :] = total
    gather_col_start(k_ref, slab, k_s, k_r, p, q)

    @pl.when(p != q)
    def _():
        remote(cp_ref.at[piece(q)], cq_ref.at[piece(p)], turn_s, turn_r, (q, p)).wait_recv()

    gather_row_start(cq_ref, cq_s, cq_r, p, q)
    gather_row_pass(cq_ref, cq_s, cq_r, p, q)
    gather_col_wait(cp_ref, piece, cp_s, cp_r, p, q)
    gather_col_wait(k_ref, slab, k_s, k_r, p, q)
    gather_row_wait(cq_ref, cq_s, cq_r, p, q)

    gather_row_drain(cq_ref, cq_s, cq_r, p, q)
    gather_col_drain(cp_ref, piece, cp_s, cp_r, p, q)
    gather_col_drain(k_ref, slab, k_s, k_r, p, q)

    @pl.when(p != q)
    def _():
        remote(cp_ref.at[piece(q)], cq_ref.at[piece(q)], turn_s, turn_r, (q, p)).wait_send()

    for i in range(1, D):
        t = lax.rem(q + i, D)
        remote(kp_ref.at[slab(t)], kparts.at[q], kp_s.at[i], kp_r.at[q], (p, t)).wait_send()
        remote(x_ref.at[piece(t)], parts.at[q], x_s.at[i], x_r.at[q], (p, t)).wait_send()
        t = lax.rem(p + i, D)
        remote(ksum, krows.at[p], kr_s.at[i], kr_r.at[p], (t, q)).wait_send()


def share_image(x, kp, middle):
    vmem = pl.BlockSpec(memory_space=pltpu.VMEM)
    tall = jax.ShapeDtypeStruct((4 * B, B), jnp.float32)
    many, one = pltpu.SemaphoreType.DMA((D,)), pltpu.SemaphoreType.DMA
    return pl.pallas_call(
        image_kernel,
        out_shape=(tall, tall, jax.ShapeDtypeStruct((B, B), jnp.float32)),
        in_specs=[vmem] * 3,
        out_specs=(vmem,) * 3,
        scratch_shapes=[
            pltpu.VMEM((D, PIECE, B), jnp.float32),
            pltpu.VMEM((D, SLICE, B), jnp.float32),
            pltpu.VMEM((SLICE, B), jnp.float32),
            pltpu.VMEM((D, SLICE, B), jnp.float32),
            many, many, many, many, many, many, many, many, many, many, one, one, many, many,
        ],
        compiler_params=pltpu.CompilerParams(
            collective_id=8, has_side_effects=True, vmem_limit_bytes=VMEM_LIMIT
        ),
        name="share_image",
    )(x, kp, middle)


def update_kernel(
    a_ref, vr_ref, cp_ref, vq_ref, cq_ref, k_ref, mid_ref, out_ref, right_high, right_low
):
    @pl.when(pl.program_id(0) == 0)
    def _():
        middle = mid_ref[...]
        shift = dot3(dot3(middle, k_ref[...], 1, 0), middle, 1, 0)
        shift = split(0.5 * (shift + shift.T))
        for tile in range(4):
            rows = slice(tile * B, tile * B + B)
            vq = vq_ref[rows, :]
            high, low = split(vq.T)
            right_high[:B, rows] = high
            right_low[:B, rows] = low
            other = cq_ref[rows, :] - dot_split(split(vq), shift, 1, 0)
            high, low = split(other.T)
            right_high[B:, rows] = high
            right_low[B:, rows] = low

    left = split(jnp.concatenate((cp_ref[...], vr_ref[...]), 1))
    out_ref[...] = a_ref[...] - dot_split(left, (right_high[...], right_low[...]), 1, 0)


def update(matrix, vr, cp, vq, cq, k, middle):
    rows = 128
    size = 4 * B
    whole = lambda shape: pl.BlockSpec(shape, lambda i: (0, 0))
    tile = lambda width: pl.BlockSpec((rows, width), lambda i: (i, 0))
    return pl.pallas_call(
        update_kernel,
        out_shape=jax.ShapeDtypeStruct((size, size), jnp.float32),
        grid=(size // rows,),
        in_specs=[
            tile(size), tile(B), tile(B), whole((size, B)), whole((size, B)),
            whole((B, B)), whole((B, B)),
        ],
        out_specs=tile(size),
        scratch_shapes=[pltpu.VMEM((2 * B, size), jnp.bfloat16)] * 2,
        compiler_params=pltpu.CompilerParams(vmem_limit_bytes=VMEM_LIMIT),
        name="update",
    )(matrix, vr, cp, vq, cq, k, middle)


def body(affinity):
    matrix = affinity
    for panel in range(PANELS):
        pr, pq, gt = share_panel(panel, matrix)
        vr, vq, middle, x, kp = factor(panel, matrix, pr, pq, gt)
        cp, cq, k = share_image(x, kp, middle)
        matrix = update(matrix, vr, cp, vq, cq, k, middle)
    return matrix


def solution(mesh):
    return jax.shard_map(
        body,
        mesh=mesh,
        in_specs=(P("row", "col"),),
        out_specs=P("row", "col"),
        check_vma=False,
    )
```

```python
import functools

import jax
import jax.numpy as jnp
from jax import lax
from jax.experimental import pallas as pl
from jax.experimental.pallas import tpu as pltpu
from jax.sharding import PartitionSpec as P

B = 256
PANELS = 2
NS_STEPS = 12
D = 16
PIECE = 64
SLICE = 16
MESH = pl.DeviceIdType.MESH
HIGHEST = lax.Precision.HIGHEST
VMEM_LIMIT = 56 * 1024 * 1024


def dot(first, second, first_dim, second_dim):
    return lax.dot_general(
        first,
        second,
        (((first_dim,), (second_dim,)), ((), ())),
        precision=HIGHEST,
        preferred_element_type=jnp.float32,
    )


def split(value):
    high = value.astype(jnp.bfloat16)
    return high, (value - high.astype(jnp.float32)).astype(jnp.bfloat16)


def dot_split(first, second, first_dim, second_dim):
    def one(x, y):
        return lax.dot_general(
            x, y, (((first_dim,), (second_dim,)), ((), ())), preferred_element_type=jnp.float32
        )

    return one(first[0], second[0]) + (one(first[0], second[1]) + one(first[1], second[0]))


def dot3(first, second, first_dim, second_dim):
    return dot_split(split(first), split(second), first_dim, second_dim)


def sublane(x, j):
    return jnp.broadcast_to(x[j : j + 1, :], x.shape)


def chol_inverse_128(d_ref):
    n = 128
    sub = lax.broadcasted_iota(jnp.int32, (8, n), 0)
    lane = lax.broadcasted_iota(jnp.int32, (8, n), 1)
    rows = [d_ref[8 * g : 8 * g + 8, :] for g in range(n // 8)]
    for g in range(n // 8):
        k0 = 8 * g
        own = (lane >= k0) & (lane < k0 + 8)
        unit = jnp.where(lane == sub + k0, 1.0, 0.0)
        cur = rows[g]
        cols = [jnp.broadcast_to(cur[:, k0 + j : k0 + j + 1], (8, n)) for j in range(8)]
        cur = jnp.where(own, unit, cur)
        recips, factors, pivots = [], {}, []
        diag = jnp.ones((8, n), jnp.float32)
        for j in range(8):
            d = sublane(cols[j], j)
            recips.append(1.0 / d)
            diag = jnp.where(sub == j, d, diag)
            f = jnp.where(sub > j, cols[j] * recips[j], 0.0)
            for l in range(j + 1, 8):
                factors[j, l] = sublane(cols[l], j)
                cols[l] = cols[l] - f * factors[j, l]
            pivots.append(sublane(cur, j))
            cur = cur - f * pivots[j]
        d_ref[k0 : k0 + 8, :] = jnp.where(lane < k0 + 8, cur, 0.0) / jnp.sqrt(diag)
        for i in range(g + 1, n // 8):
            low = rows[i]
            cols = [jnp.broadcast_to(low[:, k0 + j : k0 + j + 1], (8, n)) for j in range(8)]
            low = jnp.where(own, 0.0, low)
            for j in range(8):
                f = cols[j] * recips[j]
                for l in range(j + 1, 8):
                    cols[l] = cols[l] - f * factors[j, l]
                low = low - f * pivots[j]
            rows[i] = low


def chol_inverse(gram_ref, out_ref, d_ref, half_ref, below_ref):
    half = B // 2
    d_ref[...] = gram_ref[:half, :half]

    def step(i, carry):
        chol_inverse_128(d_ref)
        half_ref[i] = d_ref[...]

        @pl.when(i == 0)
        def _():
            below = dot(gram_ref[half:, :half], d_ref[...], 1, 1)
            below_ref[...] = below
            d_ref[...] = gram_ref[half:, half:] - dot(below, below, 1, 1)

        return carry

    lax.fori_loop(0, 2, step, 0)
    first, second = half_ref[0], half_ref[1]
    out_ref[:half, :half] = first
    out_ref[:half, half:] = jnp.zeros((half, half), jnp.float32)
    out_ref[half:, :half] = -dot(second, dot(below_ref[...], first, 1, 0), 1, 0)
    out_ref[half:, half:] = second


def eye():
    r = lax.broadcasted_iota(jnp.int32, (B, B), 0)
    c = lax.broadcasted_iota(jnp.int32, (B, B), 1)
    return jnp.where(r == c, 1.0, 0.0)


def greet(p, q):
    barrier = pltpu.get_barrier_semaphore()
    for i in range(1, D):
        pl.semaphore_signal(
            barrier, inc=1, device_id=(lax.rem(p + i, D), q), device_id_type=MESH
        )
        pl.semaphore_signal(
            barrier, inc=1, device_id=(p, lax.rem(q + i, D)), device_id_type=MESH
        )

    @pl.when(p != q)
    def _():
        pl.semaphore_signal(barrier, inc=1, device_id=(q, p), device_id_type=MESH)


def await_greetings(p, q):
    barrier = pltpu.get_barrier_semaphore()

    @pl.when(p != q)
    def _():
        pl.semaphore_wait(barrier, 2 * (D - 1) + 1)

    @pl.when(p == q)
    def _():
        pl.semaphore_wait(barrier, 2 * (D - 1))


def remote(src, dst, send, recv, target):
    return pltpu.make_async_remote_copy(
        src_ref=src, dst_ref=dst, send_sem=send, recv_sem=recv,
        device_id=target, device_id_type=MESH,
    )


def piece(index):
    return pl.ds(pl.multiple_of(index * PIECE, PIECE), PIECE)


def slab(index):
    return pl.ds(pl.multiple_of(index * SLICE, SLICE), SLICE)


def gather_col_start(ref, at, send, recv, p, q):
    for i in range(1, D):
        t = lax.rem(q + i, D)
        remote(ref.at[at(q)], ref.at[at(q)], send.at[i], recv.at[q], (p, t)).start()


def gather_col_wait(ref, at, send, recv, p, q):
    for i in range(1, D):
        t = lax.rem(q + i, D)
        remote(ref.at[at(t)], ref.at[at(t)], send.at[i], recv.at[t], (p, t)).wait_recv()


def gather_col_drain(ref, at, send, recv, p, q):
    for i in range(1, D):
        t = lax.rem(q + i, D)
        remote(ref.at[at(q)], ref.at[at(q)], send.at[i], recv.at[q], (p, t)).wait_send()


def gather_row_start(ref, send, recv, p, q):
    for i in range(0, D, 2):
        t = lax.rem(p + i, D) if i else p + 1 - 2 * lax.rem(p, 2)
        remote(ref.at[piece(p)], ref.at[piece(p)], send.at[i], recv.at[p], (t, q)).start()


def gather_row_pass(ref, send, recv, p, q):
    other = p + 1 - 2 * lax.rem(p, 2)
    for i in (2, 14, 4, 12, 6, 10, 8):
        t = lax.rem(p + i, D)
        remote(ref.at[piece(t)], ref.at[piece(t)], send.at[i], recv.at[t], (t, q)).wait_recv()
        remote(ref.at[piece(t)], ref.at[piece(t)], send.at[i + 1], recv.at[t], (other, q)).start()


def gather_row_wait(ref, send, recv, p, q):
    other = p + 1 - 2 * lax.rem(p, 2)
    for i in range(0, D, 2):
        t = lax.rem(other + i, D)
        remote(ref.at[piece(t)], ref.at[piece(t)], send.at[i], recv.at[t], (other, q)).wait_recv()


def gather_row_drain(ref, send, recv, p, q):
    other = p + 1 - 2 * lax.rem(p, 2)
    for i in range(0, D, 2):
        remote(ref.at[piece(p)], ref.at[piece(p)], send.at[i], recv.at[p], (other, q)).wait_send()
        if i:
            t = lax.rem(p + i, D)
            remote(
                ref.at[piece(t)], ref.at[piece(t)], send.at[i + 1], recv.at[t], (other, q)
            ).wait_send()


def reduce_kernel(
    panel, a_ref, vr_ref, vq_ref, cp_ref, cq_ref, k_ref, mid_ref,
    a_vm, pr_ref, pq_ref, g_ref, t_ref, tall, wide, turned, gram, part, block,
    inv_ref, d_ref, half_ref, below_ref, w_ref,
    x_ref, kp_ref, parts, kparts, ksum, kpair, khalf, kz,
    load, gram_s, gram_r, block_s, block_r, gdown_s, gdown_r, tdown_s, tdown_r,
    g_s, g_r, t_s, t_r, prs_s, prs_r, pr_s, pr_r, pqs_s, pqs_r, pq_s, pq_r,
    x_s, x_r, kp_s, kp_r, pair_s, pair_r, kz_s, kz_r, half_s, half_r, k_s, k_r,
    cp_s, cp_r, turn_s, turn_r, cq_s, cq_r,
):
    p, q = lax.axis_index("row"), lax.axis_index("col")
    row_owner, col_owner, top_col = p == panel, q == panel, q == panel + 1
    core = lax.rem(p, 2)
    other = p + 1 - 2 * core
    whole = lambda index: index
    row_peers = [lax.rem(p + i, D) for i in range(D)]
    col_peers = [lax.rem(q + i, D) for i in range(D)]

    loads = [
        pltpu.make_async_copy(a_ref.at[pl.ds(0, B)], a_vm.at[pl.ds(0, B)], load.at[0]),
        pltpu.make_async_copy(
            a_ref.at[pl.ds(B, 3 * B)], a_vm.at[pl.ds(B, 3 * B)], load.at[1]
        ),
    ]
    for copy in loads:
        copy.start()
    greet(p, q)
    loads[0].wait()

    @pl.when(row_owner)
    def _():
        wide[...] = a_vm[:B, :]

        @pl.when(q <= panel)
        def _():
            wide[:, :B] = jnp.zeros((B, B), jnp.float32)

        gram[...] = dot(wide[...], wide[...], 1, 1)

    await_greetings(p, q)

    gram_out = lambda i: remote(
        gram.at[slab(col_peers[i])], part.at[q], gram_s.at[i], gram_r.at[q], (p, col_peers[i])
    )
    block_out = lambda i: remote(
        block.at[slab(col_peers[i])], t_ref.at[col_peers[i]], block_s.at[i], block_r,
        (p, col_peers[i]),
    )
    pq_out = lambda i: remote(
        turned.at[piece(row_peers[i])], pq_ref.at[piece(row_peers[i])], pqs_s.at[i], pqs_r,
        (row_peers[i], q),
    )
    pr_out = lambda i: remote(
        tall.at[piece(col_peers[i])], pr_ref.at[piece(col_peers[i])], prs_s.at[i], prs_r,
        (p, col_peers[i]),
    )
    g_down = lambda i: remote(
        g_ref.at[q], g_ref.at[q], gdown_s.at[i], gdown_r, (row_peers[i], q)
    )
    t_down = lambda i: remote(
        t_ref.at[q], t_ref.at[q], tdown_s.at[i], tdown_r, (row_peers[i], q)
    )

    @pl.when(row_owner)
    def _():
        for i in range(1, D):
            gram_out(i).start()
        part[q] = gram[slab(q), :]

        @pl.when(top_col)
        def _():
            block[...] = wide[:, :B].T
            for i in range(1, D):
                block_out(i).start()
            t_ref[q] = block[slab(q), :]

        turned[...] = wide[...].T
        for i in range(1, D):
            pq_out(i).start()
        pq_ref[piece(p), :] = turned[piece(p), :]

    loads[1].wait()

    @pl.when(col_owner)
    def _():
        tall[...] = a_vm[:, :B]

        @pl.when(p <= panel)
        def _():
            tall[:B, :] = jnp.zeros((B, B), jnp.float32)

        for i in range(1, D):
            pr_out(i).start()
        pr_ref[piece(q), :] = tall[piece(q), :]

    @pl.when(row_owner)
    def _():
        for i in range(1, D):
            t = col_peers[i]
            remote(gram.at[slab(q)], part.at[t], gram_s.at[i], gram_r.at[t], (p, t)).wait_recv()
        total = part[0]
        for i in range(1, D):
            total = total + part[i]
        g_ref[q] = total
        for i in range(1, D):
            g_down(i).start()

        @pl.when(jnp.logical_not(top_col))
        def _():
            block_out(1).wait_recv()

        for i in range(1, D):
            t_down(i).start()

    @pl.when(jnp.logical_not(row_owner))
    def _():
        g_down(1).wait_recv()

    gather_col_start(g_ref, whole, g_s, g_r, p, q)

    @pl.when(jnp.logical_not(row_owner))
    def _():
        t_down(1).wait_recv()

    gather_col_start(t_ref, whole, t_s, t_r, p, q)

    @pl.when(jnp.logical_not(row_owner))
    def _():
        pq_out(1).wait_recv()

    gather_row_start(pq_ref, pq_s, pq_r, p, q)

    @pl.when(jnp.logical_not(col_owner))
    def _():
        pr_out(1).wait_recv()

    gather_col_start(pr_ref, piece, pr_s, pr_r, p, q)

    gather_col_wait(g_ref, whole, g_s, g_r, p, q)
    kp_ref[...] = g_ref[...].reshape(B, B)
    chol_inverse(kp_ref, inv_ref, d_ref, half_ref, below_ref)
    gather_row_pass(pq_ref, pq_s, pq_r, p, q)
    gather_col_wait(t_ref, whole, t_s, t_r, p, q)
    inverse_low = inv_ref[...]
    top = dot(t_ref[...].reshape(B, B), inverse_low, 1, 1)
    w_ref[...] = top

    def polar_step(i, carry):
        w = w_ref[...]
        s = split(w)
        w_ref[...] = 1.5 * w - 0.5 * dot_split(s, split(dot_split(s, s, 0, 0)), 1, 0)
        return carry

    lax.fori_loop(0, NS_STEPS, polar_step, 0)
    w = w_ref[...]
    cross = dot(w, top, 0, 0)
    metric = eye() + cross + cross.T + dot(w, w, 0, 0)
    guess = (40.0 / 41.0) * eye() - (8.0 / 41.0) * metric
    for i in range(4):
        mul = dot if i == 3 else dot3
        guess = guess + mul(guess, eye() - mul(metric, guess, 1, 0), 1, 0)
    mid_ref[...] = 2.0 * guess

    gather_row_wait(pq_ref, pq_s, pq_r, p, q)
    inv_split = split(inverse_low)

    def reflect(ref, out):
        def step(tile, carry):
            rows = pl.ds(pl.multiple_of(tile * B, B), B)
            out[rows, :] = dot_split(split(ref[rows, :]), inv_split, 1, 1)
            return carry

        lax.fori_loop(0, 4, step, 0)

    reflect(pq_ref, vq_ref)

    @pl.when(top_col)
    def _():
        vq_ref[:B, :] = vq_ref[:B, :] + w

    gather_col_wait(pr_ref, piece, pr_s, pr_r, p, q)
    reflect(pr_ref, vr_ref)

    @pl.when(p == panel + 1)
    def _():
        vr_ref[:B, :] = vr_ref[:B, :] + w_ref[...]

    vq = split(vq_ref[...])
    kp_ref[...] = jnp.zeros((B, B), jnp.float32)
    x_out = lambda t: remote(
        x_ref.at[piece(t)], parts.at[q], x_s.at[t], x_r.at[q], (p, t)
    )

    def product_step(number, carry):
        tile = lax.rem(q // 4 + number, 4)
        rows = pl.ds(pl.multiple_of(tile * B, B), B)
        x = dot_split(split(a_vm[rows, :]), vq, 1, 0)
        x_ref[rows, :] = x
        for i in range(4):
            t = 4 * tile + lax.rem(q + i, 4)

            @pl.when(t != q)
            def _():
                x_out(t).start()

        kp_ref[...] += dot3(vr_ref[rows, :], x, 0, 0)
        return carry

    lax.fori_loop(0, 4, product_step, 0)
    parts[q] = x_ref[piece(q), :]
    kp_out = lambda i: remote(
        kp_ref.at[slab(col_peers[i])], kparts.at[q], kp_s.at[i], kp_r.at[q], (p, col_peers[i])
    )
    for i in range(1, D):
        kp_out(i).start()
    kparts[q] = kp_ref[slab(q), :]

    for i in range(1, D):
        t = col_peers[i]
        remote(x_ref.at[piece(q)], parts.at[t], x_s.at[t], x_r.at[t], (p, t)).wait_recv()
    total = parts[0]
    for i in range(1, D):
        total = total + parts[i]
    image = dot(total, mid_ref[...], 1, 0)
    cp_ref[piece(q), :] = image
    turn_out = remote(cp_ref.at[piece(q)], cq_ref.at[piece(q)], turn_s, turn_r, (q, p))

    @pl.when(p != q)
    def _():
        turn_out.start()

    @pl.when(p == q)
    def _():
        cq_ref[piece(p), :] = image

    gather_col_start(cp_ref, piece, cp_s, cp_r, p, q)

    for i in range(1, D):
        t = col_peers[i]
        remote(kp_ref.at[slab(q)], kparts.at[t], kp_s.at[i], kp_r.at[t], (p, t)).wait_recv()
    total = kparts[0]
    for i in range(1, D):
        total = total + kparts[i]
    ksum[...] = total
    pair_out = remote(ksum, kpair, pair_s, pair_r, (other, q))
    pair_out.start()
    pair_out.wait_recv()
    khalf[...] = ksum[...] + kpair[...]
    mine = pl.ds(pl.multiple_of(core * 8, 8), 8)
    kz_out = lambda i: remote(
        khalf.at[mine], kz.at[p // 2], kz_s.at[i // 2], kz_r.at[p // 2], (row_peers[i], q)
    )
    for i in range(2, D, 2):
        kz_out(i).start()
    kz[p // 2] = khalf[mine, :]

    @pl.when(p != q)
    def _():
        remote(cp_ref.at[piece(q)], cq_ref.at[piece(p)], turn_s, turn_r, (q, p)).wait_recv()

    gather_row_start(cq_ref, cq_s, cq_r, p, q)
    for i in range(2, D, 2):
        t = row_peers[i] // 2
        remote(
            khalf.at[mine], kz.at[t], kz_s.at[i // 2], kz_r.at[t], (row_peers[i], q)
        ).wait_recv()
    total = kz[0]
    for i in range(1, D // 2):
        total = total + kz[i]
    here = pl.ds(pl.multiple_of(q * SLICE + core * 8, 8), 8)
    there = pl.ds(pl.multiple_of(q * SLICE + 8 - core * 8, 8), 8)
    k_ref[here, :] = total
    half_out = remote(k_ref.at[here], k_ref.at[here], half_s, half_r, (other, q))
    half_out.start()
    remote(k_ref.at[there], k_ref.at[there], half_s, half_r, (other, q)).wait_recv()
    gather_col_start(k_ref, slab, k_s, k_r, p, q)
    gather_row_pass(cq_ref, cq_s, cq_r, p, q)
    gather_col_wait(cp_ref, piece, cp_s, cp_r, p, q)
    gather_col_wait(k_ref, slab, k_s, k_r, p, q)
    gather_row_wait(cq_ref, cq_s, cq_r, p, q)

    gather_row_drain(cq_ref, cq_s, cq_r, p, q)
    gather_row_drain(pq_ref, pq_s, pq_r, p, q)
    for ref, at, send, recv in (
        (cp_ref, piece, cp_s, cp_r), (k_ref, slab, k_s, k_r), (pr_ref, piece, pr_s, pr_r),
        (g_ref, whole, g_s, g_r), (t_ref, whole, t_s, t_r),
    ):
        gather_col_drain(ref, at, send, recv, p, q)

    @pl.when(p != q)
    def _():
        turn_out.wait_send()

    pair_out.wait_send()
    half_out.wait_send()
    for i in range(2, D, 2):
        kz_out(i).wait_send()
    for i in range(1, D):
        kp_out(i).wait_send()
        x_out(col_peers[i]).wait_send()

    @pl.when(row_owner)
    def _():
        for i in range(1, D):
            gram_out(i).wait_send()
            pq_out(i).wait_send()
            g_down(i).wait_send()
            t_down(i).wait_send()

        @pl.when(top_col)
        def _():
            for i in range(1, D):
                block_out(i).wait_send()

    @pl.when(col_owner)
    def _():
        for i in range(1, D):
            pr_out(i).wait_send()


def reduce_panel(panel, matrix):
    vmem = pl.BlockSpec(memory_space=pltpu.VMEM)
    buffer = lambda *shape: pltpu.VMEM(shape, jnp.float32)
    tall = jax.ShapeDtypeStruct((4 * B, B), jnp.float32)
    square = jax.ShapeDtypeStruct((B, B), jnp.float32)
    many, one = pltpu.SemaphoreType.DMA((D,)), pltpu.SemaphoreType.DMA
    return pl.pallas_call(
        functools.partial(reduce_kernel, panel),
        out_shape=(tall, tall, tall, tall, square, square),
        in_specs=[pl.BlockSpec(memory_space=pl.ANY)],
        out_specs=(vmem,) * 6,
        scratch_shapes=[
            buffer(4 * B, 4 * B), buffer(4 * B, B), buffer(4 * B, B),
            buffer(D, SLICE, B), buffer(D, SLICE, B),
            buffer(4 * B, B), buffer(B, 4 * B), buffer(4 * B, B),
            buffer(B, B), buffer(D, SLICE, B), buffer(B, B),
            buffer(B, B), buffer(B // 2, B // 2), buffer(2, B // 2, B // 2),
            buffer(B // 2, B // 2), buffer(B, B),
            buffer(4 * B, B), buffer(B, B), buffer(D, PIECE, B), buffer(D, SLICE, B),
            buffer(SLICE, B), buffer(SLICE, B), buffer(SLICE, B), buffer(D // 2, 8, B),
            pltpu.SemaphoreType.DMA((2,)),
            many, many, many, one, many, one, many, one,
            many, many, many, many, many, one, many, many, many, one, many, many,
            many, many, many, many, one, one, many, many, one, one, many, many,
            many, many, one, one, many, many,
        ],
        compiler_params=pltpu.CompilerParams(
            collective_id=1 + panel, has_side_effects=True, vmem_limit_bytes=VMEM_LIMIT
        ),
        name=f"reduce_panel_{panel}",
    )(matrix)


def update_kernel(
    a_ref, vr_ref, cp_ref, vq_ref, cq_ref, k_ref, mid_ref, out_ref, right_high, right_low
):
    @pl.when(pl.program_id(0) == 0)
    def _():
        middle = mid_ref[...]
        shift = dot3(dot3(middle, k_ref[...], 1, 0), middle, 1, 0)
        shift = split(0.5 * (shift + shift.T))
        for tile in range(4):
            rows = slice(tile * B, tile * B + B)
            vq = vq_ref[rows, :]
            high, low = split(vq.T)
            right_high[:B, rows] = high
            right_low[:B, rows] = low
            other = cq_ref[rows, :] - dot_split(split(vq), shift, 1, 0)
            high, low = split(other.T)
            right_high[B:, rows] = high
            right_low[B:, rows] = low

    left = split(jnp.concatenate((cp_ref[...], vr_ref[...]), 1))
    out_ref[...] = a_ref[...] - dot_split(left, (right_high[...], right_low[...]), 1, 0)


def update(matrix, vr, cp, vq, cq, k, middle):
    rows = 128
    size = 4 * B
    whole = lambda shape: pl.BlockSpec(shape, lambda i: (0, 0))
    tile = lambda width: pl.BlockSpec((rows, width), lambda i: (i, 0))
    return pl.pallas_call(
        update_kernel,
        out_shape=jax.ShapeDtypeStruct((size, size), jnp.float32),
        grid=(size // rows,),
        in_specs=[
            tile(size), tile(B), tile(B), whole((size, B)), whole((size, B)),
            whole((B, B)), whole((B, B)),
        ],
        out_specs=tile(size),
        scratch_shapes=[pltpu.VMEM((2 * B, size), jnp.bfloat16)] * 2,
        compiler_params=pltpu.CompilerParams(vmem_limit_bytes=VMEM_LIMIT),
        name="update",
    )(matrix, vr, cp, vq, cq, k, middle)


def body(affinity):
    matrix = affinity
    for panel in range(PANELS):
        vr, vq, cp, cq, k, middle = reduce_panel(panel, matrix)
        matrix = update(matrix, vr, cp, vq, cq, k, middle)
    return matrix


def solution(mesh):
    return jax.shard_map(
        body,
        mesh=mesh,
        in_specs=(P("row", "col"),),
        out_specs=P("row", "col"),
        check_vma=False,
    )
```

```python
import types

import jax
import jax.numpy as jnp
from jax import lax
from jax.experimental import pallas as pl
from jax.experimental.pallas import tpu as pltpu
from jax.sharding import PartitionSpec as P

B = 256
PANELS = 2
NS_STEPS = 12
D = 16
PIECE = 64
SLICE = 16
MESH = pl.DeviceIdType.MESH
HIGHEST = lax.Precision.HIGHEST
VMEM_LIMIT = 56 * 1024 * 1024


def dot(first, second, first_dim, second_dim):
    return lax.dot_general(
        first,
        second,
        (((first_dim,), (second_dim,)), ((), ())),
        precision=HIGHEST,
        preferred_element_type=jnp.float32,
    )


def split(value):
    high = value.astype(jnp.bfloat16)
    return high, (value - high.astype(jnp.float32)).astype(jnp.bfloat16)


def dot_split(first, second, first_dim, second_dim):
    def one(x, y):
        return lax.dot_general(
            x, y, (((first_dim,), (second_dim,)), ((), ())), preferred_element_type=jnp.float32
        )

    return one(first[0], second[0]) + (one(first[0], second[1]) + one(first[1], second[0]))


def dot3(first, second, first_dim, second_dim):
    return dot_split(split(first), split(second), first_dim, second_dim)


def sublane(x, j):
    return jnp.broadcast_to(x[j : j + 1, :], x.shape)


def chol_inverse_128(d_ref):
    n = 128
    sub = lax.broadcasted_iota(jnp.int32, (8, n), 0)
    lane = lax.broadcasted_iota(jnp.int32, (8, n), 1)
    rows = [d_ref[8 * g : 8 * g + 8, :] for g in range(n // 8)]
    for g in range(n // 8):
        k0 = 8 * g
        own = (lane >= k0) & (lane < k0 + 8)
        unit = jnp.where(lane == sub + k0, 1.0, 0.0)
        cur = rows[g]
        cols = [jnp.broadcast_to(cur[:, k0 + j : k0 + j + 1], (8, n)) for j in range(8)]
        cur = jnp.where(own, unit, cur)
        recips, factors, pivots = [], {}, []
        diag = jnp.ones((8, n), jnp.float32)
        for j in range(8):
            d = sublane(cols[j], j)
            recips.append(1.0 / d)
            diag = jnp.where(sub == j, d, diag)
            f = jnp.where(sub > j, cols[j] * recips[j], 0.0)
            for l in range(j + 1, 8):
                factors[j, l] = sublane(cols[l], j)
                cols[l] = cols[l] - f * factors[j, l]
            pivots.append(sublane(cur, j))
            cur = cur - f * pivots[j]
        d_ref[k0 : k0 + 8, :] = jnp.where(lane < k0 + 8, cur, 0.0) / jnp.sqrt(diag)
        for i in range(g + 1, n // 8):
            low = rows[i]
            cols = [jnp.broadcast_to(low[:, k0 + j : k0 + j + 1], (8, n)) for j in range(8)]
            low = jnp.where(own, 0.0, low)
            for j in range(8):
                f = cols[j] * recips[j]
                for l in range(j + 1, 8):
                    cols[l] = cols[l] - f * factors[j, l]
                low = low - f * pivots[j]
            rows[i] = low


def chol_inverse(gram_ref, out_ref, d_ref, half_ref, below_ref):
    half = B // 2
    d_ref[...] = gram_ref[:half, :half]

    def step(i, carry):
        chol_inverse_128(d_ref)
        half_ref[i] = d_ref[...]

        @pl.when(i == 0)
        def _():
            below = dot(gram_ref[half:, :half], d_ref[...], 1, 1)
            below_ref[...] = below
            d_ref[...] = gram_ref[half:, half:] - dot(below, below, 1, 1)

        return carry

    lax.fori_loop(0, 2, step, 0)
    first, second = half_ref[0], half_ref[1]
    out_ref[:half, :half] = first
    out_ref[:half, half:] = jnp.zeros((half, half), jnp.float32)
    out_ref[half:, :half] = -dot(second, dot(below_ref[...], first, 1, 0), 1, 0)
    out_ref[half:, half:] = second


def eye():
    r = lax.broadcasted_iota(jnp.int32, (B, B), 0)
    c = lax.broadcasted_iota(jnp.int32, (B, B), 1)
    return jnp.where(r == c, 1.0, 0.0)


def greet(p, q):
    barrier = pltpu.get_barrier_semaphore()
    for i in range(1, D):
        pl.semaphore_signal(
            barrier, inc=1, device_id=(lax.rem(p + i, D), q), device_id_type=MESH
        )
        pl.semaphore_signal(
            barrier, inc=1, device_id=(p, lax.rem(q + i, D)), device_id_type=MESH
        )

    @pl.when(p != q)
    def _():
        pl.semaphore_signal(barrier, inc=1, device_id=(q, p), device_id_type=MESH)


def await_greetings(p, q):
    barrier = pltpu.get_barrier_semaphore()

    @pl.when(p != q)
    def _():
        pl.semaphore_wait(barrier, 2 * (D - 1) + 1)

    @pl.when(p == q)
    def _():
        pl.semaphore_wait(barrier, 2 * (D - 1))


def remote(src, dst, send, recv, target):
    return pltpu.make_async_remote_copy(
        src_ref=src, dst_ref=dst, send_sem=send, recv_sem=recv,
        device_id=target, device_id_type=MESH,
    )


def piece(index):
    return pl.ds(pl.multiple_of(index * PIECE, PIECE), PIECE)


def slab(index):
    return pl.ds(pl.multiple_of(index * SLICE, SLICE), SLICE)


def gather_col_start(ref, at, send, recv, p, q):
    for i in range(1, D):
        t = lax.rem(q + i, D)
        remote(ref.at[at(q)], ref.at[at(q)], send.at[i], recv.at[q], (p, t)).start()


def gather_col_wait(ref, at, send, recv, p, q):
    for i in range(1, D):
        t = lax.rem(q + i, D)
        remote(ref.at[at(t)], ref.at[at(t)], send.at[i], recv.at[t], (p, t)).wait_recv()


def gather_col_drain(ref, at, send, recv, p, q):
    for i in range(1, D):
        t = lax.rem(q + i, D)
        remote(ref.at[at(q)], ref.at[at(q)], send.at[i], recv.at[q], (p, t)).wait_send()


def gather_row_start(ref, send, recv, p, q):
    for i in range(0, D, 2):
        t = lax.rem(p + i, D) if i else p + 1 - 2 * lax.rem(p, 2)
        remote(ref.at[piece(p)], ref.at[piece(p)], send.at[i], recv.at[p], (t, q)).start()


def gather_row_pass(ref, send, recv, p, q, number=None):
    other = p + 1 - 2 * lax.rem(p, 2)
    order = ((2, 14), (4, 12), (6, 10), (8,))
    for i in sum(order, ()) if number is None else order[number]:
        t = lax.rem(p + i, D)
        remote(ref.at[piece(t)], ref.at[piece(t)], send.at[i], recv.at[t], (t, q)).wait_recv()
        remote(ref.at[piece(t)], ref.at[piece(t)], send.at[i + 1], recv.at[t], (other, q)).start()


def gather_row_wait(ref, send, recv, p, q):
    other = p + 1 - 2 * lax.rem(p, 2)
    for i in range(0, D, 2):
        t = lax.rem(other + i, D)
        remote(ref.at[piece(t)], ref.at[piece(t)], send.at[i], recv.at[t], (other, q)).wait_recv()


def gather_row_drain(ref, send, recv, p, q):
    other = p + 1 - 2 * lax.rem(p, 2)
    for i in range(0, D, 2):
        remote(ref.at[piece(p)], ref.at[piece(p)], send.at[i], recv.at[p], (other, q)).wait_send()
        if i:
            t = lax.rem(p + i, D)
            remote(
                ref.at[piece(t)], ref.at[piece(t)], send.at[i + 1], recv.at[t], (other, q)
            ).wait_send()


TALL, SQUARE, SLABS = (4 * B, B), (B, B), (D, SLICE, B)
PANEL_BUFFERS = dict(
    pr_ref=TALL, pq_ref=TALL, g_ref=SLABS, t_ref=SLABS, tall=TALL, wide=(B, 4 * B), turned=TALL,
    gram=SQUARE, part=SLABS, block=SQUARE, x_ref=TALL, kp_ref=SQUARE, parts=(D, PIECE, B),
    kparts=SLABS, ksum=(SLICE, B), kpair=(SLICE, B), khalf=(SLICE, B), kz=(D // 2, 8, B),
    cp_ref=TALL, cq_ref=TALL, k_ref=SQUARE,
)
PANEL_MANY = (
    "gram_s", "gram_r", "block_s", "gdown_s", "tdown_s", "g_s", "g_r", "t_s", "t_r", "prs_s",
    "pr_s", "pr_r", "pqs_s", "pq_s", "pq_r", "x_s", "x_r", "kp_s", "kp_r", "kz_s", "kz_r",
    "k_s", "k_r", "cp_s", "cp_r", "cq_s", "cq_r",
)
PANEL_ONE = (
    "block_r", "gdown_r", "tdown_r", "prs_r", "pqs_r", "pair_s", "pair_r", "half_s", "half_r",
    "turn_s", "turn_r",
)
LOCAL_BUFFERS = dict(
    a_vm=(4 * B, 4 * B), vq_ref=TALL, mid_ref=SQUARE, inv_ref=SQUARE, d_ref=(B // 2, B // 2),
    half_ref=(2, B // 2, B // 2), below_ref=(B // 2, B // 2), w_ref=SQUARE,
)


def tile_rows(tile):
    return pl.ds(pl.multiple_of(tile * B, B), B)


def reduce_kernel(a_ref, a_out, vr_ref, last_high, last_low, *scratch):
    scratch = list(scratch)
    take = lambda names: {name: scratch.pop(0) for name in names}
    local = types.SimpleNamespace(a_ref=a_ref, a_out=a_out, vr_ref=vr_ref, **take(LOCAL_BUFFERS))
    local.last = (last_high, last_low)
    local.turned_vq = (scratch.pop(0), scratch.pop(0))
    local.load, local.store = scratch.pop(0), scratch.pop(0)
    sets = [
        types.SimpleNamespace(**take(PANEL_BUFFERS), **take(PANEL_MANY), **take(PANEL_ONE))
        for _ in range(PANELS)
    ]
    local.loads = [
        pltpu.make_async_copy(
            a_ref.at[pl.ds(0, B)], local.a_vm.at[pl.ds(0, B)], local.load.at[0]
        ),
        pltpu.make_async_copy(
            a_ref.at[pl.ds(B, 3 * B)], local.a_vm.at[pl.ds(B, 3 * B)], local.load.at[1]
        ),
    ]
    for copy in local.loads:
        copy.start()
    greet(lax.axis_index("row"), lax.axis_index("col"))
    local.loads[0].wait()
    drains = [one_panel(panel, local, sets[panel]) for panel in range(PANELS)]
    for drain in drains:
        drain()
    pltpu.make_async_copy(local.a_vm, a_out, local.store).wait()


def subtract(a_vm, left, right, rows):
    a_vm[rows, :] -= dot_split(split(left[rows, :]), (right[0][...], right[1][...]), 1, 0)


def one_panel(panel, local, refs):
    a_vm, vr_ref, vq_ref, mid_ref = local.a_vm, local.vr_ref, local.vq_ref, local.mid_ref
    inv_ref, w_ref = local.inv_ref, local.w_ref
    pr_ref, pq_ref, g_ref, t_ref = refs.pr_ref, refs.pq_ref, refs.g_ref, refs.t_ref
    tall, wide, turned, gram = refs.tall, refs.wide, refs.turned, refs.gram
    part, block, x_ref, kp_ref = refs.part, refs.block, refs.x_ref, refs.kp_ref
    parts, kparts, ksum, kpair = refs.parts, refs.kparts, refs.ksum, refs.kpair
    khalf, kz, cp_ref, cq_ref = refs.khalf, refs.kz, refs.cp_ref, refs.cq_ref
    k_ref, gram_s, gram_r, block_s = refs.k_ref, refs.gram_s, refs.gram_r, refs.block_s
    gdown_s, tdown_s, g_s, g_r = refs.gdown_s, refs.tdown_s, refs.g_s, refs.g_r
    t_s, t_r, prs_s, pr_s = refs.t_s, refs.t_r, refs.prs_s, refs.pr_s
    pr_r, pqs_s, pq_s, pq_r = refs.pr_r, refs.pqs_s, refs.pq_s, refs.pq_r
    x_s, x_r, kp_s, kp_r = refs.x_s, refs.x_r, refs.kp_s, refs.kp_r
    kz_s, kz_r, k_s, k_r = refs.kz_s, refs.kz_r, refs.k_s, refs.k_r
    cp_s, cp_r, cq_s, cq_r = refs.cp_s, refs.cp_r, refs.cq_s, refs.cq_r
    block_r, gdown_r, tdown_r, prs_r = refs.block_r, refs.gdown_r, refs.tdown_r, refs.prs_r
    pqs_r, pair_s, pair_r, half_s = refs.pqs_r, refs.pair_s, refs.pair_r, refs.half_s
    half_r, turn_s, turn_r = refs.half_r, refs.turn_s, refs.turn_r
    p, q = lax.axis_index("row"), lax.axis_index("col")
    row_owner, col_owner, top_col = p == panel, q == panel, q == panel + 1
    core = lax.rem(p, 2)
    other = p + 1 - 2 * core
    whole = lambda index: index
    row_peers = [lax.rem(p + i, D) for i in range(D)]
    col_peers = [lax.rem(q + i, D) for i in range(D)]

    @pl.when(row_owner)
    def _():
        wide[...] = a_vm[:B, :]

        @pl.when(q <= panel)
        def _():
            wide[:, :B] = jnp.zeros((B, B), jnp.float32)

        gram[...] = dot(wide[...], wide[...], 1, 1)

    if panel == 0:
        await_greetings(p, q)

    gram_out = lambda i: remote(
        gram.at[slab(col_peers[i])], part.at[q], gram_s.at[i], gram_r.at[q], (p, col_peers[i])
    )
    block_out = lambda i: remote(
        block.at[slab(col_peers[i])], t_ref.at[col_peers[i]], block_s.at[i], block_r,
        (p, col_peers[i]),
    )
    pq_out = lambda i: remote(
        turned.at[piece(row_peers[i])], pq_ref.at[piece(row_peers[i])], pqs_s.at[i], pqs_r,
        (row_peers[i], q),
    )
    pr_out = lambda i: remote(
        tall.at[piece(col_peers[i])], pr_ref.at[piece(col_peers[i])], prs_s.at[i], prs_r,
        (p, col_peers[i]),
    )
    g_down = lambda i: remote(
        g_ref.at[q], g_ref.at[q], gdown_s.at[i], gdown_r, (row_peers[i], q)
    )
    t_down = lambda i: remote(
        t_ref.at[q], t_ref.at[q], tdown_s.at[i], tdown_r, (row_peers[i], q)
    )

    @pl.when(row_owner)
    def _():
        for i in range(1, D):
            gram_out(i).start()
        part[q] = gram[slab(q), :]

        @pl.when(top_col)
        def _():
            block[...] = wide[:, :B].T
            for i in range(1, D):
                block_out(i).start()
            t_ref[q] = block[slab(q), :]

        turned[...] = wide[...].T
        for i in range(1, D):
            pq_out(i).start()
        pq_ref[piece(p), :] = turned[piece(p), :]

    if panel == 0:
        local.loads[1].wait()
    else:
        for tile in range(1, 4):
            subtract(a_vm, vr_ref, local.last, slice(tile * B, tile * B + B))

    @pl.when(col_owner)
    def _():
        tall[...] = a_vm[:, :B]

        @pl.when(p <= panel)
        def _():
            tall[:B, :] = jnp.zeros((B, B), jnp.float32)

        for i in range(1, D):
            pr_out(i).start()
        pr_ref[piece(q), :] = tall[piece(q), :]

    @pl.when(row_owner)
    def _():
        for i in range(1, D):
            t = col_peers[i]
            remote(gram.at[slab(q)], part.at[t], gram_s.at[i], gram_r.at[t], (p, t)).wait_recv()
        total = part[0]
        for i in range(1, D):
            total = total + part[i]
        g_ref[q] = total
        for i in range(1, D):
            g_down(i).start()

        @pl.when(jnp.logical_not(top_col))
        def _():
            block_out(1).wait_recv()

        for i in range(1, D):
            t_down(i).start()

    @pl.when(jnp.logical_not(row_owner))
    def _():
        g_down(1).wait_recv()

    gather_col_start(g_ref, whole, g_s, g_r, p, q)

    @pl.when(jnp.logical_not(row_owner))
    def _():
        t_down(1).wait_recv()

    gather_col_start(t_ref, whole, t_s, t_r, p, q)

    @pl.when(jnp.logical_not(row_owner))
    def _():
        pq_out(1).wait_recv()

    gather_row_start(pq_ref, pq_s, pq_r, p, q)

    @pl.when(jnp.logical_not(col_owner))
    def _():
        pr_out(1).wait_recv()

    gather_col_start(pr_ref, piece, pr_s, pr_r, p, q)

    gather_col_wait(g_ref, whole, g_s, g_r, p, q)
    kp_ref[...] = g_ref[...].reshape(B, B)
    chol_inverse(kp_ref, inv_ref, local.d_ref, local.half_ref, local.below_ref)
    gather_row_pass(pq_ref, pq_s, pq_r, p, q)
    gather_col_wait(t_ref, whole, t_s, t_r, p, q)
    inverse_low = inv_ref[...]
    top = dot(t_ref[...].reshape(B, B), inverse_low, 1, 1)
    w_ref[...] = top

    def polar_step(i, carry):
        w = w_ref[...]
        s = split(w)
        w_ref[...] = 1.5 * w - 0.5 * dot_split(split(dot_split(s, s, 1, 1)), s, 1, 0)
        return carry

    lax.fori_loop(0, NS_STEPS, polar_step, 0)
    w = w_ref[...]
    cross = dot(w, top, 0, 0)
    metric = eye() + cross + cross.T + dot(w, w, 0, 0)
    guess = (40.0 / 41.0) * eye() - (8.0 / 41.0) * metric
    for i in range(4):
        mul = dot if i == 3 else dot3
        guess = guess + mul(guess, eye() - mul(metric, guess, 1, 0), 1, 0)
    mid_ref[...] = 2.0 * guess

    gather_row_wait(pq_ref, pq_s, pq_r, p, q)
    inv_split = split(inverse_low)

    def reflect(ref, out):
        def step(tile, carry):
            rows = pl.ds(pl.multiple_of(tile * B, B), B)
            out[rows, :] = dot_split(split(ref[rows, :]), inv_split, 1, 1)
            return carry

        lax.fori_loop(0, 4, step, 0)

    reflect(pq_ref, vq_ref)

    @pl.when(top_col)
    def _():
        vq_ref[:B, :] = vq_ref[:B, :] + w

    gather_col_wait(pr_ref, piece, pr_s, pr_r, p, q)
    reflect(pr_ref, vr_ref)

    @pl.when(p == panel + 1)
    def _():
        vr_ref[:B, :] = vr_ref[:B, :] + w_ref[...]

    vq = split(vq_ref[...])
    kp_ref[...] = jnp.zeros((B, B), jnp.float32)
    x_out = lambda t: remote(
        x_ref.at[piece(t)], parts.at[q], x_s.at[t], x_r.at[q], (p, t)
    )

    def product_step(number, carry):
        tile = lax.rem(q // 4 + number, 4)
        rows = pl.ds(pl.multiple_of(tile * B, B), B)
        x = dot_split(split(a_vm[rows, :]), vq, 1, 0)
        x_ref[rows, :] = x
        for i in range(4):
            t = 4 * tile + lax.rem(q + i, 4)

            @pl.when(t != q)
            def _():
                x_out(t).start()

        kp_ref[...] += dot3(vr_ref[rows, :], x, 0, 0)
        return carry

    lax.fori_loop(0, 4, product_step, 0)
    parts[q] = x_ref[piece(q), :]
    kp_out = lambda i: remote(
        kp_ref.at[slab(col_peers[i])], kparts.at[q], kp_s.at[i], kp_r.at[q], (p, col_peers[i])
    )
    for i in range(1, D):
        kp_out(i).start()
    kparts[q] = kp_ref[slab(q), :]

    for tile in range(4):
        rows = slice(tile * B, tile * B + B)
        local.turned_vq[0][:, rows], local.turned_vq[1][:, rows] = split(vq_ref[rows, :].T)

    for i in range(1, D):
        t = col_peers[i]
        remote(x_ref.at[piece(q)], parts.at[t], x_s.at[t], x_r.at[t], (p, t)).wait_recv()
    total = parts[0]
    for i in range(1, D):
        total = total + parts[i]
    image = dot(total, mid_ref[...], 1, 0)
    cp_ref[piece(q), :] = image
    turn_out = remote(cp_ref.at[piece(q)], cq_ref.at[piece(q)], turn_s, turn_r, (q, p))

    @pl.when(p != q)
    def _():
        turn_out.start()

    @pl.when(p == q)
    def _():
        cq_ref[piece(p), :] = image

    gather_col_start(cp_ref, piece, cp_s, cp_r, p, q)

    for i in range(1, D):
        t = col_peers[i]
        remote(kp_ref.at[slab(q)], kparts.at[t], kp_s.at[i], kp_r.at[t], (p, t)).wait_recv()
    total = kparts[0]
    for i in range(1, D):
        total = total + kparts[i]
    ksum[...] = total
    pair_out = remote(ksum, kpair, pair_s, pair_r, (other, q))
    pair_out.start()
    pair_out.wait_recv()
    khalf[...] = ksum[...] + kpair[...]
    mine = pl.ds(pl.multiple_of(core * 8, 8), 8)
    kz_out = lambda i: remote(
        khalf.at[mine], kz.at[p // 2], kz_s.at[i // 2], kz_r.at[p // 2], (row_peers[i], q)
    )
    for i in range(2, D, 2):
        kz_out(i).start()
    kz[p // 2] = khalf[mine, :]

    @pl.when(p != q)
    def _():
        remote(cp_ref.at[piece(q)], cq_ref.at[piece(p)], turn_s, turn_r, (q, p)).wait_recv()

    gather_row_start(cq_ref, cq_s, cq_r, p, q)
    for i in range(2, D, 2):
        t = row_peers[i] // 2
        remote(
            khalf.at[mine], kz.at[t], kz_s.at[i // 2], kz_r.at[t], (row_peers[i], q)
        ).wait_recv()
    total = kz[0]
    for i in range(1, D // 2):
        total = total + kz[i]
    here = pl.ds(pl.multiple_of(q * SLICE + core * 8, 8), 8)
    there = pl.ds(pl.multiple_of(q * SLICE + 8 - core * 8, 8), 8)
    k_ref[here, :] = total
    half_out = remote(k_ref.at[here], k_ref.at[here], half_s, half_r, (other, q))
    half_out.start()
    remote(k_ref.at[there], k_ref.at[there], half_s, half_r, (other, q)).wait_recv()
    gather_col_start(k_ref, slab, k_s, k_r, p, q)
    for number in range(4):
        tile = lax.rem(q // 4 + number, 4)
        for i in range(4):
            t = 4 * tile + lax.rem(q + i, 4)

            @pl.when(t != q)
            def _():
                remote(
                    cp_ref.at[piece(t)], cp_ref.at[piece(t)], cp_s.at[0], cp_r.at[t], (p, t)
                ).wait_recv()

        subtract(a_vm, cp_ref, local.turned_vq, tile_rows(tile))
        gather_row_pass(cq_ref, cq_s, cq_r, p, q, number)
    if panel == PANELS - 1:
        pltpu.make_async_copy(a_vm, local.a_out, local.store).start()
    gather_col_wait(k_ref, slab, k_s, k_r, p, q)
    middle = mid_ref[...]
    shift = dot3(dot3(middle, k_ref[...], 1, 0), middle, 1, 0)
    shift = split(0.5 * (shift + shift.T))
    gather_row_wait(cq_ref, cq_s, cq_r, p, q)
    for tile in range(4):
        rows = slice(tile * B, tile * B + B)
        rest = cq_ref[rows, :] - dot_split(split(vq_ref[rows, :]), shift, 1, 0)
        local.last[0][:, rows], local.last[1][:, rows] = split(rest.T)
    if panel < PANELS - 1:
        subtract(a_vm, vr_ref, local.last, slice(0, B))

    def drain():
        gather_row_drain(cq_ref, cq_s, cq_r, p, q)
        gather_row_drain(pq_ref, pq_s, pq_r, p, q)
        for ref, at, send, recv in (
            (cp_ref, piece, cp_s, cp_r), (k_ref, slab, k_s, k_r), (pr_ref, piece, pr_s, pr_r),
            (g_ref, whole, g_s, g_r), (t_ref, whole, t_s, t_r),
        ):
            gather_col_drain(ref, at, send, recv, p, q)

        @pl.when(p != q)
        def _():
            turn_out.wait_send()

        pair_out.wait_send()
        half_out.wait_send()
        for i in range(2, D, 2):
            kz_out(i).wait_send()
        for i in range(1, D):
            kp_out(i).wait_send()
            x_out(col_peers[i]).wait_send()

        @pl.when(row_owner)
        def _():
            for i in range(1, D):
                gram_out(i).wait_send()
                pq_out(i).wait_send()
                g_down(i).wait_send()
                t_down(i).wait_send()

            @pl.when(top_col)
            def _():
                for i in range(1, D):
                    block_out(i).wait_send()

        @pl.when(col_owner)
        def _():
            for i in range(1, D):
                pr_out(i).wait_send()

    return drain


def reduce_panels(matrix):
    vmem, anywhere = pl.BlockSpec(memory_space=pltpu.VMEM), pl.BlockSpec(memory_space=pl.ANY)
    buffers = lambda shapes: [pltpu.VMEM(shape, jnp.float32) for shape in shapes.values()]
    many, one = pltpu.SemaphoreType.DMA((D,)), pltpu.SemaphoreType.DMA
    right = jax.ShapeDtypeStruct((B, 4 * B), jnp.bfloat16)
    panel_set = buffers(PANEL_BUFFERS) + [many] * len(PANEL_MANY) + [one] * len(PANEL_ONE)
    return pl.pallas_call(
        reduce_kernel,
        out_shape=(
            jax.ShapeDtypeStruct((4 * B, 4 * B), jnp.float32),
            jax.ShapeDtypeStruct(TALL, jnp.float32), right, right,
        ),
        in_specs=[anywhere],
        out_specs=(anywhere, vmem, vmem, vmem),
        scratch_shapes=buffers(LOCAL_BUFFERS)
        + [pltpu.VMEM((B, 4 * B), jnp.bfloat16)] * 2
        + [pltpu.SemaphoreType.DMA((2,)), one]
        + panel_set * PANELS,
        compiler_params=pltpu.CompilerParams(
            collective_id=1, has_side_effects=True, vmem_limit_bytes=VMEM_LIMIT
        ),
        name="reduce_panels",
    )(matrix)


def finish_kernel(a_ref, vr_ref, high_ref, low_ref, out_ref):
    out_ref[...] = a_ref[...] - dot_split(
        split(vr_ref[...]), (high_ref[...], low_ref[...]), 1, 0
    )


def finish(matrix, vr, high, low):
    rows, size = 128, 4 * B
    tile = lambda width: pl.BlockSpec((rows, width), lambda i: (i, 0))
    whole = pl.BlockSpec((B, size), lambda i: (0, 0))
    return pl.pallas_call(
        finish_kernel,
        out_shape=jax.ShapeDtypeStruct((size, size), jnp.float32),
        grid=(size // rows,),
        in_specs=[tile(size), tile(B), whole, whole],
        out_specs=tile(size),
        compiler_params=pltpu.CompilerParams(vmem_limit_bytes=VMEM_LIMIT),
        name="finish",
    )(matrix, vr, high, low)


def body(affinity):
    return finish(*reduce_panels(affinity))


def solution(mesh):
    return jax.shard_map(
        body,
        mesh=mesh,
        in_specs=(P("row", "col"),),
        out_specs=P("row", "col"),
        check_vma=False,
    )
```

```python
import types

import jax
import jax.numpy as jnp
from jax import lax
from jax.experimental import pallas as pl
from jax.experimental.pallas import tpu as pltpu
from jax.sharding import PartitionSpec as P

B = 256
PANELS = 2
NS_STEPS = 12
D = 16
PIECE = 64
SLICE = 16
MESH = pl.DeviceIdType.MESH
HIGHEST = lax.Precision.HIGHEST
VMEM_LIMIT = 56 * 1024 * 1024


def dot(first, second, first_dim, second_dim):
    return lax.dot_general(
        first,
        second,
        (((first_dim,), (second_dim,)), ((), ())),
        precision=HIGHEST,
        preferred_element_type=jnp.float32,
    )


def split(value):
    high = value.astype(jnp.bfloat16)
    return high, (value - high.astype(jnp.float32)).astype(jnp.bfloat16)


def dot_split(first, second, first_dim, second_dim):
    def one(x, y):
        return lax.dot_general(
            x, y, (((first_dim,), (second_dim,)), ((), ())), preferred_element_type=jnp.float32
        )

    return one(first[0], second[0]) + (one(first[0], second[1]) + one(first[1], second[0]))


def dot3(first, second, first_dim, second_dim):
    return dot_split(split(first), split(second), first_dim, second_dim)


def sublane(x, j):
    return jnp.broadcast_to(x[j : j + 1, :], x.shape)


def chol_inverse_128(d_ref):
    n = 128
    sub = lax.broadcasted_iota(jnp.int32, (8, n), 0)
    lane = lax.broadcasted_iota(jnp.int32, (8, n), 1)
    rows = [d_ref[8 * g : 8 * g + 8, :] for g in range(n // 8)]
    for g in range(n // 8):
        k0 = 8 * g
        own = (lane >= k0) & (lane < k0 + 8)
        unit = jnp.where(lane == sub + k0, 1.0, 0.0)
        cur = rows[g]
        cols = [jnp.broadcast_to(cur[:, k0 + j : k0 + j + 1], (8, n)) for j in range(8)]
        cur = jnp.where(own, unit, cur)
        recips, factors, pivots = [], {}, []
        diag = jnp.ones((8, n), jnp.float32)
        for j in range(8):
            d = sublane(cols[j], j)
            recips.append(1.0 / d)
            diag = jnp.where(sub == j, d, diag)
            f = cols[j] * recips[j]
            for l in range(j + 1, 8):
                factors[j, l] = sublane(cols[l], j)
                cols[l] = cols[l] - f * factors[j, l]
            pivots.append(sublane(cur, j))
            cur = cur - jnp.where(sub > j, f, 0.0) * pivots[j]
        d_ref[k0 : k0 + 8, :] = jnp.where(lane < k0 + 8, cur, 0.0) / jnp.sqrt(diag)
        for i in range(g + 1, n // 8):
            low = rows[i]
            cols = [jnp.broadcast_to(low[:, k0 + j : k0 + j + 1], (8, n)) for j in range(8)]
            low = jnp.where(own, 0.0, low)
            for j in range(8):
                f = cols[j] * recips[j]
                for l in range(j + 1, 8):
                    cols[l] = cols[l] - f * factors[j, l]
                low = low - f * pivots[j]
            rows[i] = low


def chol_inverse(gram_ref, out_ref, d_ref, half_ref, below_ref):
    half = B // 2
    d_ref[...] = gram_ref[:half, :half]

    def step(i, carry):
        chol_inverse_128(d_ref)
        half_ref[i] = d_ref[...]

        @pl.when(i == 0)
        def _():
            below = dot(gram_ref[half:, :half], d_ref[...], 1, 1)
            below_ref[...] = below
            d_ref[...] = gram_ref[half:, half:] - dot(below, below, 1, 1)

        return carry

    lax.fori_loop(0, 2, step, 0)
    first, second = half_ref[0], half_ref[1]
    out_ref[:half, :half] = first
    out_ref[:half, half:] = jnp.zeros((half, half), jnp.float32)
    out_ref[half:, :half] = -dot(second, dot(below_ref[...], first, 1, 0), 1, 0)
    out_ref[half:, half:] = second


def eye():
    r = lax.broadcasted_iota(jnp.int32, (B, B), 0)
    c = lax.broadcasted_iota(jnp.int32, (B, B), 1)
    return jnp.where(r == c, 1.0, 0.0)


def greet(p, q):
    barrier = pltpu.get_barrier_semaphore()
    for i in range(1, D):
        pl.semaphore_signal(
            barrier, inc=1, device_id=(lax.rem(p + i, D), q), device_id_type=MESH
        )
        pl.semaphore_signal(
            barrier, inc=1, device_id=(p, lax.rem(q + i, D)), device_id_type=MESH
        )

    @pl.when(p != q)
    def _():
        pl.semaphore_signal(barrier, inc=1, device_id=(q, p), device_id_type=MESH)


def await_greetings(p, q):
    barrier = pltpu.get_barrier_semaphore()

    @pl.when(p != q)
    def _():
        pl.semaphore_wait(barrier, 2 * (D - 1) + 1)

    @pl.when(p == q)
    def _():
        pl.semaphore_wait(barrier, 2 * (D - 1))


def remote(src, dst, send, recv, target):
    return pltpu.make_async_remote_copy(
        src_ref=src, dst_ref=dst, send_sem=send, recv_sem=recv,
        device_id=target, device_id_type=MESH,
    )


def piece(index):
    return pl.ds(pl.multiple_of(index * PIECE, PIECE), PIECE)


def half_piece(half):
    size = PIECE // 2
    return lambda index: pl.ds(pl.multiple_of(index * PIECE + half * size, size), size)


HALVES = (half_piece(0), half_piece(1))


def slab(index):
    return pl.ds(pl.multiple_of(index * SLICE, SLICE), SLICE)


def gather_col_start(ref, at, send, recv, p, q):
    for i in range(1, D):
        t = lax.rem(q + i, D)
        remote(ref.at[at(q)], ref.at[at(q)], send.at[i], recv.at[q], (p, t)).start()


def gather_col_wait(ref, at, send, recv, p, q):
    for i in range(1, D):
        t = lax.rem(q + i, D)
        remote(ref.at[at(t)], ref.at[at(t)], send.at[i], recv.at[t], (p, t)).wait_recv()


def gather_col_drain(ref, at, send, recv, p, q):
    for i in range(1, D):
        t = lax.rem(q + i, D)
        remote(ref.at[at(q)], ref.at[at(q)], send.at[i], recv.at[q], (p, t)).wait_send()


def gather_row_start(ref, send, recv, p, q, at=None):
    at = at or piece
    for i in range(0, D, 2):
        t = lax.rem(p + i, D) if i else p + 1 - 2 * lax.rem(p, 2)
        remote(ref.at[at(p)], ref.at[at(p)], send.at[i], recv.at[p], (t, q)).start()


def gather_row_pass(ref, send, recv, p, q, number=None, at=None):
    other = p + 1 - 2 * lax.rem(p, 2)
    order = ((2, 14), (4, 12), (6, 10), (8,))
    at = at or piece
    for i in sum(order, ()) if number is None else order[number]:
        t = lax.rem(p + i, D)
        remote(ref.at[at(t)], ref.at[at(t)], send.at[i], recv.at[t], (t, q)).wait_recv()
        remote(ref.at[at(t)], ref.at[at(t)], send.at[i + 1], recv.at[t], (other, q)).start()


def gather_row_wait(ref, send, recv, p, q, at=None):
    other = p + 1 - 2 * lax.rem(p, 2)
    at = at or piece
    for i in range(0, D, 2):
        t = lax.rem(other + i, D)
        remote(ref.at[at(t)], ref.at[at(t)], send.at[i], recv.at[t], (other, q)).wait_recv()


def gather_row_drain(ref, send, recv, p, q, at=None):
    other = p + 1 - 2 * lax.rem(p, 2)
    at = at or piece
    for i in range(0, D, 2):
        remote(ref.at[at(p)], ref.at[at(p)], send.at[i], recv.at[p], (other, q)).wait_send()
        if i:
            t = lax.rem(p + i, D)
            remote(
                ref.at[at(t)], ref.at[at(t)], send.at[i + 1], recv.at[t], (other, q)
            ).wait_send()


TALL, SQUARE, SLABS = (4 * B, B), (B, B), (D, SLICE, B)
PANEL_BUFFERS = dict(
    pr_ref=TALL, pq_ref=TALL, g_ref=SLABS, t_ref=SLABS, tall=TALL, wide=(B, 4 * B), turned=TALL,
    gram=SQUARE, part=SLABS, block=SQUARE, x_ref=TALL, kp_ref=SQUARE, parts=(D, PIECE, B),
    kparts=SLABS, ksum=(SLICE, B), kpair=(SLICE, B), khalf=(SLICE, B), kz=(D // 2, 8, B),
    cp_ref=TALL, cq_ref=TALL, k_ref=SQUARE,
)
PANEL_MANY = (
    "gram_s", "gram_r", "block_s", "gdown_s", "tdown_s", "g_s", "g_r", "t_s", "t_r", "prs_s",
    "pr_s", "pr_r", "pqs_s", "pq_s", "pq_r", "x_s", "x_r", "kp_s", "kp_r", "kz_s", "kz_r",
    "k_s", "k_r", "cp_s", "cp_r", "cq_s", "cq_r",
    "x2_s", "x2_r", "cp2_s", "cp2_r", "cq2_s", "cq2_r",
)
PANEL_ONE = (
    "block_r", "gdown_r", "tdown_r", "prs_r", "pqs_r", "pair_s", "pair_r", "half_s", "half_r",
    "turn_s", "turn_r", "turn2_s", "turn2_r",
)
LOCAL_BUFFERS = dict(
    a_vm=(4 * B, 4 * B), vq_ref=TALL, mid_ref=SQUARE, inv_ref=SQUARE, d_ref=(B // 2, B // 2),
    half_ref=(2, B // 2, B // 2), below_ref=(B // 2, B // 2), w_ref=SQUARE,
)


def tile_rows(tile):
    return pl.ds(pl.multiple_of(tile * B, B), B)


def reduce_kernel(a_ref, a_out, vr_ref, last_high, last_low, *scratch):
    scratch = list(scratch)
    take = lambda names: {name: scratch.pop(0) for name in names}
    local = types.SimpleNamespace(a_ref=a_ref, a_out=a_out, vr_ref=vr_ref, **take(LOCAL_BUFFERS))
    local.last = (last_high, last_low)
    local.turned_vq = (scratch.pop(0), scratch.pop(0))
    local.load, local.store = scratch.pop(0), scratch.pop(0)
    sets = [
        types.SimpleNamespace(**take(PANEL_BUFFERS), **take(PANEL_MANY), **take(PANEL_ONE))
        for _ in range(PANELS)
    ]
    local.loads = [
        pltpu.make_async_copy(
            a_ref.at[pl.ds(0, B)], local.a_vm.at[pl.ds(0, B)], local.load.at[0]
        ),
        pltpu.make_async_copy(
            a_ref.at[pl.ds(B, 3 * B)], local.a_vm.at[pl.ds(B, 3 * B)], local.load.at[1]
        ),
    ]
    for copy in local.loads:
        copy.start()
    greet(lax.axis_index("row"), lax.axis_index("col"))
    local.loads[0].wait()
    drains = [one_panel(panel, local, sets[panel]) for panel in range(PANELS)]
    for drain in drains:
        drain()
    pltpu.make_async_copy(local.a_vm, a_out, local.store).wait()


def subtract(a_vm, left, right, rows):
    a_vm[rows, :] -= dot_split(split(left[rows, :]), (right[0][...], right[1][...]), 1, 0)


def one_panel(panel, local, refs):
    a_vm, vr_ref, vq_ref, mid_ref = local.a_vm, local.vr_ref, local.vq_ref, local.mid_ref
    inv_ref, w_ref = local.inv_ref, local.w_ref
    pr_ref, pq_ref, g_ref, t_ref = refs.pr_ref, refs.pq_ref, refs.g_ref, refs.t_ref
    tall, wide, turned, gram = refs.tall, refs.wide, refs.turned, refs.gram
    part, block, x_ref, kp_ref = refs.part, refs.block, refs.x_ref, refs.kp_ref
    parts, kparts, ksum, kpair = refs.parts, refs.kparts, refs.ksum, refs.kpair
    khalf, kz, cp_ref, cq_ref = refs.khalf, refs.kz, refs.cp_ref, refs.cq_ref
    k_ref, gram_s, gram_r, block_s = refs.k_ref, refs.gram_s, refs.gram_r, refs.block_s
    gdown_s, tdown_s, g_s, g_r = refs.gdown_s, refs.tdown_s, refs.g_s, refs.g_r
    t_s, t_r, prs_s, pr_s = refs.t_s, refs.t_r, refs.prs_s, refs.pr_s
    pr_r, pqs_s, pq_s, pq_r = refs.pr_r, refs.pqs_s, refs.pq_s, refs.pq_r
    kp_s, kp_r = refs.kp_s, refs.kp_r
    kz_s, kz_r, k_s, k_r = refs.kz_s, refs.kz_r, refs.k_s, refs.k_r
    x_sems = ((refs.x_s, refs.x_r), (refs.x2_s, refs.x2_r))
    cp_sems = ((refs.cp_s, refs.cp_r), (refs.cp2_s, refs.cp2_r))
    cq_sems = ((refs.cq_s, refs.cq_r), (refs.cq2_s, refs.cq2_r))
    turn_sems = ((refs.turn_s, refs.turn_r), (refs.turn2_s, refs.turn2_r))
    block_r, gdown_r, tdown_r, prs_r = refs.block_r, refs.gdown_r, refs.tdown_r, refs.prs_r
    pqs_r, pair_s, pair_r, half_s = refs.pqs_r, refs.pair_s, refs.pair_r, refs.half_s
    half_r = refs.half_r
    p, q = lax.axis_index("row"), lax.axis_index("col")
    row_owner, col_owner, top_col = p == panel, q == panel, q == panel + 1
    core = lax.rem(p, 2)
    other = p + 1 - 2 * core
    whole = lambda index: index
    row_peers = [lax.rem(p + i, D) for i in range(D)]
    col_peers = [lax.rem(q + i, D) for i in range(D)]

    @pl.when(row_owner)
    def _():
        wide[...] = a_vm[:B, :]

        @pl.when(q <= panel)
        def _():
            wide[:, :B] = jnp.zeros((B, B), jnp.float32)

        gram[...] = dot(wide[...], wide[...], 1, 1)

    if panel == 0:
        await_greetings(p, q)

    gram_out = lambda i: remote(
        gram.at[slab(col_peers[i])], part.at[q], gram_s.at[i], gram_r.at[q], (p, col_peers[i])
    )
    block_out = lambda i: remote(
        block.at[slab(col_peers[i])], t_ref.at[col_peers[i]], block_s.at[i], block_r,
        (p, col_peers[i]),
    )
    pq_out = lambda i: remote(
        turned.at[piece(row_peers[i])], pq_ref.at[piece(row_peers[i])], pqs_s.at[i], pqs_r,
        (row_peers[i], q),
    )
    pr_out = lambda i: remote(
        tall.at[piece(col_peers[i])], pr_ref.at[piece(col_peers[i])], prs_s.at[i], prs_r,
        (p, col_peers[i]),
    )
    g_down = lambda i: remote(
        g_ref.at[q], g_ref.at[q], gdown_s.at[i], gdown_r, (row_peers[i], q)
    )
    t_down = lambda i: remote(
        t_ref.at[q], t_ref.at[q], tdown_s.at[i], tdown_r, (row_peers[i], q)
    )

    @pl.when(row_owner)
    def _():
        for i in range(1, D):
            gram_out(i).start()
        part[q] = gram[slab(q), :]

        @pl.when(top_col)
        def _():
            block[...] = wide[:, :B].T
            for i in range(1, D):
                block_out(i).start()
            t_ref[q] = block[slab(q), :]

        turned[...] = wide[...].T
        for i in range(1, D):
            pq_out(i).start()
        pq_ref[piece(p), :] = turned[piece(p), :]

    if panel == 0:
        local.loads[1].wait()
    else:
        for tile in range(1, 4):
            subtract(a_vm, vr_ref, local.last, slice(tile * B, tile * B + B))

    @pl.when(col_owner)
    def _():
        tall[...] = a_vm[:, :B]

        @pl.when(p <= panel)
        def _():
            tall[:B, :] = jnp.zeros((B, B), jnp.float32)

        for i in range(1, D):
            pr_out(i).start()
        pr_ref[piece(q), :] = tall[piece(q), :]

    @pl.when(row_owner)
    def _():
        for i in range(1, D):
            t = col_peers[i]
            remote(gram.at[slab(q)], part.at[t], gram_s.at[i], gram_r.at[t], (p, t)).wait_recv()
        total = part[0]
        for i in range(1, D):
            total = total + part[i]
        g_ref[q] = total
        for i in range(1, D):
            g_down(i).start()

        @pl.when(jnp.logical_not(top_col))
        def _():
            block_out(1).wait_recv()

        for i in range(1, D):
            t_down(i).start()

    @pl.when(jnp.logical_not(row_owner))
    def _():
        g_down(1).wait_recv()

    gather_col_start(g_ref, whole, g_s, g_r, p, q)

    @pl.when(jnp.logical_not(row_owner))
    def _():
        t_down(1).wait_recv()

    gather_col_start(t_ref, whole, t_s, t_r, p, q)

    @pl.when(jnp.logical_not(row_owner))
    def _():
        pq_out(1).wait_recv()

    gather_row_start(pq_ref, pq_s, pq_r, p, q)

    gather_col_wait(g_ref, whole, g_s, g_r, p, q)

    @pl.when(jnp.logical_not(col_owner))
    def _():
        pr_out(1).wait_recv()

    gather_col_start(pr_ref, piece, pr_s, pr_r, p, q)

    kp_ref[...] = g_ref[...].reshape(B, B)
    chol_inverse(kp_ref, inv_ref, local.d_ref, local.half_ref, local.below_ref)
    gather_row_pass(pq_ref, pq_s, pq_r, p, q)
    gather_col_wait(t_ref, whole, t_s, t_r, p, q)
    inverse_low = inv_ref[...]
    top = dot(t_ref[...].reshape(B, B), inverse_low, 1, 1)
    w_ref[...] = top

    def polar_step(i, carry):
        w = w_ref[...]
        s = split(w)
        w_ref[...] = 1.5 * w - 0.5 * dot_split(split(dot_split(s, s, 1, 1)), s, 1, 0)
        return carry

    lax.fori_loop(0, NS_STEPS, polar_step, 0)
    w = w_ref[...]
    w_split = split(w)
    cross = dot_split(w_split, split(top), 0, 0)
    metric = eye() + cross + cross.T + dot_split(w_split, w_split, 0, 0)
    guess = (40.0 / 41.0) * eye() - (8.0 / 41.0) * metric
    for i in range(4):
        guess = guess + dot3(guess, eye() - dot3(metric, guess, 1, 0), 1, 0)
    mid_ref[...] = 2.0 * guess

    gather_row_wait(pq_ref, pq_s, pq_r, p, q)
    inv_split = split(inverse_low)

    def reflect(ref, out):
        def step(tile, carry):
            rows = pl.ds(pl.multiple_of(tile * B, B), B)
            out[rows, :] = dot_split(split(ref[rows, :]), inv_split, 1, 1)
            return carry

        lax.fori_loop(0, 4, step, 0)

    reflect(pq_ref, vq_ref)

    @pl.when(top_col)
    def _():
        vq_ref[:B, :] = vq_ref[:B, :] + w

    gather_col_wait(pr_ref, piece, pr_s, pr_r, p, q)
    reflect(pr_ref, vr_ref)

    @pl.when(p == panel + 1)
    def _():
        vr_ref[:B, :] = vr_ref[:B, :] + w_ref[...]

    vq = split(vq_ref[...])
    inner = [slice(0, PIECE // 2), slice(PIECE // 2, PIECE)]
    within = [pl.ds(0, PIECE // 2), pl.ds(PIECE // 2, PIECE // 2)]

    def x_out(t, h):
        send, recv = x_sems[h]
        return remote(
            x_ref.at[HALVES[h](t)], parts.at[q, within[h]], send.at[t], recv.at[q], (p, t)
        )

    def product_step(number, carry):
        tile = lax.rem(q // 4 + number, 4)
        rows = pl.ds(pl.multiple_of(tile * B, B), B)
        x = dot_split(split(a_vm[rows, :]), vq, 1, 0)
        x_ref[rows, :] = x
        for i in range(4):
            t = 4 * tile + lax.rem(q + i, 4)

            @pl.when(t != q)
            def _():
                x_out(t, 0).start()

        return carry

    lax.fori_loop(0, 4, product_step, 0)
    for i in range(1, D):
        x_out(col_peers[i], 1).start()
    kp_ref[...] = dot3(vr_ref[...], x_ref[...], 0, 0)
    parts[q] = x_ref[piece(q), :]
    kp_out = lambda i: remote(
        kp_ref.at[slab(col_peers[i])], kparts.at[q], kp_s.at[i], kp_r.at[q], (p, col_peers[i])
    )
    for i in range(1, D):
        kp_out(i).start()
    kparts[q] = kp_ref[slab(q), :]

    for tile in range(4):
        rows = slice(tile * B, tile * B + B)
        local.turned_vq[0][:, rows], local.turned_vq[1][:, rows] = split(vq_ref[rows, :].T)

    def turn_out(h):
        send, recv = turn_sems[h]
        return remote(cp_ref.at[HALVES[h](q)], cq_ref.at[HALVES[h](q)], send, recv, (q, p))

    def turn_in(h):
        send, recv = turn_sems[h]

        @pl.when(p != q)
        def _():
            remote(
                cp_ref.at[HALVES[h](q)], cq_ref.at[HALVES[h](p)], send, recv, (q, p)
            ).wait_recv()

        gather_row_start(cq_ref, *cq_sems[h], p, q, at=HALVES[h])

    def image_half(h):
        send, recv = x_sems[h]
        for i in range(1, D):
            t = col_peers[i]
            remote(
                x_ref.at[HALVES[h](q)], parts.at[t, within[h]], send.at[t], recv.at[t], (p, t)
            ).wait_recv()
        total = parts[0, inner[h]]
        for i in range(1, D):
            total = total + parts[i, inner[h]]
        image = dot(total, mid_ref[...], 1, 0)
        cp_ref[HALVES[h](q), :] = image

        @pl.when(p != q)
        def _():
            turn_out(h).start()

        @pl.when(p == q)
        def _():
            cq_ref[HALVES[h](p), :] = image

        gather_col_start(cp_ref, HALVES[h], *cp_sems[h], p, q)

    image_half(0)
    image_half(1)
    turn_in(0)

    for i in range(1, D):
        t = col_peers[i]
        remote(kp_ref.at[slab(q)], kparts.at[t], kp_s.at[i], kp_r.at[t], (p, t)).wait_recv()
    total = kparts[0]
    for i in range(1, D):
        total = total + kparts[i]
    ksum[...] = total
    pair_out = remote(ksum, kpair, pair_s, pair_r, (other, q))
    pair_out.start()
    pair_out.wait_recv()
    khalf[...] = ksum[...] + kpair[...]
    mine = pl.ds(pl.multiple_of(core * 8, 8), 8)
    kz_out = lambda i: remote(
        khalf.at[mine], kz.at[p // 2], kz_s.at[i // 2], kz_r.at[p // 2], (row_peers[i], q)
    )
    for i in range(2, D, 2):
        kz_out(i).start()
    kz[p // 2] = khalf[mine, :]

    turn_in(1)
    for i in range(2, D, 2):
        t = row_peers[i] // 2
        remote(
            khalf.at[mine], kz.at[t], kz_s.at[i // 2], kz_r.at[t], (row_peers[i], q)
        ).wait_recv()
    total = kz[0]
    for i in range(1, D // 2):
        total = total + kz[i]
    here = pl.ds(pl.multiple_of(q * SLICE + core * 8, 8), 8)
    there = pl.ds(pl.multiple_of(q * SLICE + 8 - core * 8, 8), 8)
    k_ref[here, :] = total
    half_out = remote(k_ref.at[here], k_ref.at[here], half_s, half_r, (other, q))
    half_out.start()
    remote(k_ref.at[there], k_ref.at[there], half_s, half_r, (other, q)).wait_recv()
    gather_col_start(k_ref, slab, k_s, k_r, p, q)
    for number in range(4):
        tile = lax.rem(q // 4 + number, 4)
        for i in range(4):
            t = 4 * tile + lax.rem(q + i, 4)

            @pl.when(t != q)
            def _():
                for at, (send, recv) in zip(HALVES, cp_sems):
                    remote(
                        cp_ref.at[at(t)], cp_ref.at[at(t)], send.at[0], recv.at[t], (p, t)
                    ).wait_recv()

        subtract(a_vm, cp_ref, local.turned_vq, tile_rows(tile))
        for at, sems in zip(HALVES, cq_sems):
            gather_row_pass(cq_ref, *sems, p, q, number, at=at)
    if panel == PANELS - 1:
        pltpu.make_async_copy(a_vm, local.a_out, local.store).start()
    gather_col_wait(k_ref, slab, k_s, k_r, p, q)
    middle = mid_ref[...]
    shift = dot3(dot3(middle, k_ref[...], 1, 0), middle, 1, 0)
    shift = split(0.5 * (shift + shift.T))
    for at, sems in zip(HALVES, cq_sems):
        gather_row_wait(cq_ref, *sems, p, q, at=at)
    for tile in range(4):
        rows = slice(tile * B, tile * B + B)
        rest = cq_ref[rows, :] - dot_split(split(vq_ref[rows, :]), shift, 1, 0)
        local.last[0][:, rows], local.last[1][:, rows] = split(rest.T)
    if panel < PANELS - 1:
        subtract(a_vm, vr_ref, local.last, slice(0, B))

    def drain():
        for h in range(2):
            gather_row_drain(cq_ref, *cq_sems[h], p, q, at=HALVES[h])
            gather_col_drain(cp_ref, HALVES[h], *cp_sems[h], p, q)
        gather_row_drain(pq_ref, pq_s, pq_r, p, q)
        for ref, at, send, recv in (
            (k_ref, slab, k_s, k_r), (pr_ref, piece, pr_s, pr_r),
            (g_ref, whole, g_s, g_r), (t_ref, whole, t_s, t_r),
        ):
            gather_col_drain(ref, at, send, recv, p, q)

        @pl.when(p != q)
        def _():
            turn_out(0).wait_send()
            turn_out(1).wait_send()

        pair_out.wait_send()
        half_out.wait_send()
        for i in range(2, D, 2):
            kz_out(i).wait_send()
        for i in range(1, D):
            kp_out(i).wait_send()
            x_out(col_peers[i], 0).wait_send()
            x_out(col_peers[i], 1).wait_send()

        @pl.when(row_owner)
        def _():
            for i in range(1, D):
                gram_out(i).wait_send()
                pq_out(i).wait_send()
                g_down(i).wait_send()
                t_down(i).wait_send()

            @pl.when(top_col)
            def _():
                for i in range(1, D):
                    block_out(i).wait_send()

        @pl.when(col_owner)
        def _():
            for i in range(1, D):
                pr_out(i).wait_send()

    return drain


def reduce_panels(matrix):
    vmem, anywhere = pl.BlockSpec(memory_space=pltpu.VMEM), pl.BlockSpec(memory_space=pl.ANY)
    buffers = lambda shapes: [pltpu.VMEM(shape, jnp.float32) for shape in shapes.values()]
    many, one = pltpu.SemaphoreType.DMA((D,)), pltpu.SemaphoreType.DMA
    right = jax.ShapeDtypeStruct((B, 4 * B), jnp.bfloat16)
    panel_set = buffers(PANEL_BUFFERS) + [many] * len(PANEL_MANY) + [one] * len(PANEL_ONE)
    return pl.pallas_call(
        reduce_kernel,
        out_shape=(
            jax.ShapeDtypeStruct((4 * B, 4 * B), jnp.float32),
            jax.ShapeDtypeStruct(TALL, jnp.float32), right, right,
        ),
        in_specs=[anywhere],
        out_specs=(anywhere, vmem, vmem, vmem),
        scratch_shapes=buffers(LOCAL_BUFFERS)
        + [pltpu.VMEM((B, 4 * B), jnp.bfloat16)] * 2
        + [pltpu.SemaphoreType.DMA((2,)), one]
        + panel_set * PANELS,
        compiler_params=pltpu.CompilerParams(
            collective_id=1, has_side_effects=True, vmem_limit_bytes=VMEM_LIMIT
        ),
        name="reduce_panels",
    )(matrix)


def finish_kernel(a_ref, vr_ref, high_ref, low_ref, out_ref):
    out_ref[...] = a_ref[...] - dot_split(
        split(vr_ref[...]), (high_ref[...], low_ref[...]), 1, 0
    )


def finish(matrix, vr, high, low):
    rows, size = B, 4 * B
    tile = lambda width: pl.BlockSpec((rows, width), lambda i: (i, 0))
    whole = pl.BlockSpec((B, size), lambda i: (0, 0))
    return pl.pallas_call(
        finish_kernel,
        out_shape=jax.ShapeDtypeStruct((size, size), jnp.float32),
        grid=(size // rows,),
        in_specs=[tile(size), tile(B), whole, whole],
        out_specs=tile(size),
        compiler_params=pltpu.CompilerParams(vmem_limit_bytes=VMEM_LIMIT),
        name="finish",
    )(matrix, vr, high, low)


def body(affinity):
    return finish(*reduce_panels(affinity))


def solution(mesh):
    return jax.shard_map(
        body,
        mesh=mesh,
        in_specs=(P("row", "col"),),
        out_specs=P("row", "col"),
        check_vma=False,
    )
```

```python
import types

import jax
import jax.numpy as jnp
from jax import lax
from jax.experimental import pallas as pl
from jax.experimental.pallas import tpu as pltpu
from jax.sharding import PartitionSpec as P

B = 256
PANELS = 2
NS_STEPS = 12
D = 16
PIECE = 64
SLICE = 16
MESH = pl.DeviceIdType.MESH
HIGHEST = lax.Precision.HIGHEST
VMEM_LIMIT = 56 * 1024 * 1024


def dot(first, second, first_dim, second_dim):
    return lax.dot_general(
        first,
        second,
        (((first_dim,), (second_dim,)), ((), ())),
        precision=HIGHEST,
        preferred_element_type=jnp.float32,
    )


def split(value):
    high = value.astype(jnp.bfloat16)
    return high, (value - high.astype(jnp.float32)).astype(jnp.bfloat16)


def dot_split(first, second, first_dim, second_dim):
    def one(x, y):
        return lax.dot_general(
            x, y, (((first_dim,), (second_dim,)), ((), ())), preferred_element_type=jnp.float32
        )

    return one(first[0], second[0]) + (one(first[0], second[1]) + one(first[1], second[0]))


def dot3(first, second, first_dim, second_dim):
    return dot_split(split(first), split(second), first_dim, second_dim)


def sublane(x, j):
    return jnp.broadcast_to(x[j : j + 1, :], x.shape)


def chol_inverse_128(d_ref):
    n = 128
    sub = lax.broadcasted_iota(jnp.int32, (8, n), 0)
    lane = lax.broadcasted_iota(jnp.int32, (8, n), 1)
    rows = [d_ref[8 * g : 8 * g + 8, :] for g in range(n // 8)]
    for g in range(n // 8):
        k0 = 8 * g
        own = (lane >= k0) & (lane < k0 + 8)
        unit = jnp.where(lane == sub + k0, 1.0, 0.0)
        cur = rows[g]
        cols = [jnp.broadcast_to(cur[:, k0 + j : k0 + j + 1], (8, n)) for j in range(8)]
        cur = jnp.where(own, unit, cur)
        recips, factors, pivots = [], {}, []
        diag = jnp.ones((8, n), jnp.float32)
        for j in range(8):
            d = sublane(cols[j], j)
            recips.append(1.0 / d)
            diag = jnp.where(sub == j, d, diag)
            f = cols[j] * recips[j]
            for l in range(j + 1, 8):
                factors[j, l] = sublane(cols[l], j)
                cols[l] = cols[l] - f * factors[j, l]
            pivots.append(sublane(cur, j))
            cur = cur - jnp.where(sub > j, f, 0.0) * pivots[j]
        d_ref[k0 : k0 + 8, :] = jnp.where(lane < k0 + 8, cur, 0.0) / jnp.sqrt(diag)
        for i in range(g + 1, n // 8):
            low = rows[i]
            cols = [jnp.broadcast_to(low[:, k0 + j : k0 + j + 1], (8, n)) for j in range(8)]
            low = jnp.where(own, 0.0, low)
            for j in range(8):
                f = cols[j] * recips[j]
                for l in range(j + 1, 8):
                    cols[l] = cols[l] - f * factors[j, l]
                low = low - f * pivots[j]
            rows[i] = low


def chol_inverse(gram_ref, out_ref, d_ref, half_ref, below_ref):
    half = B // 2
    d_ref[...] = gram_ref[:half, :half]

    def step(i, carry):
        chol_inverse_128(d_ref)
        half_ref[i] = d_ref[...]

        @pl.when(i == 0)
        def _():
            below = dot(gram_ref[half:, :half], d_ref[...], 1, 1)
            below_ref[...] = below
            d_ref[...] = gram_ref[half:, half:] - dot(below, below, 1, 1)

        return carry

    lax.fori_loop(0, 2, step, 0)
    first, second = half_ref[0], half_ref[1]
    out_ref[:half, :half] = first
    out_ref[:half, half:] = jnp.zeros((half, half), jnp.float32)
    out_ref[half:, :half] = -dot(second, dot(below_ref[...], first, 1, 0), 1, 0)
    out_ref[half:, half:] = second


def eye():
    r = lax.broadcasted_iota(jnp.int32, (B, B), 0)
    c = lax.broadcasted_iota(jnp.int32, (B, B), 1)
    return jnp.where(r == c, 1.0, 0.0)


def greet(p, q):
    barrier = pltpu.get_barrier_semaphore()
    for i in range(1, D):
        pl.semaphore_signal(
            barrier, inc=1, device_id=(lax.rem(p + i, D), q), device_id_type=MESH
        )
        pl.semaphore_signal(
            barrier, inc=1, device_id=(p, lax.rem(q + i, D)), device_id_type=MESH
        )

    @pl.when(p != q)
    def _():
        pl.semaphore_signal(barrier, inc=1, device_id=(q, p), device_id_type=MESH)


def await_greetings(p, q):
    barrier = pltpu.get_barrier_semaphore()

    @pl.when(p != q)
    def _():
        pl.semaphore_wait(barrier, 2 * (D - 1) + 1)

    @pl.when(p == q)
    def _():
        pl.semaphore_wait(barrier, 2 * (D - 1))


def remote(src, dst, send, recv, target):
    return pltpu.make_async_remote_copy(
        src_ref=src, dst_ref=dst, send_sem=send, recv_sem=recv,
        device_id=target, device_id_type=MESH,
    )


def piece(index):
    return pl.ds(pl.multiple_of(index * PIECE, PIECE), PIECE)


def half_piece(half):
    size = PIECE // 2
    return lambda index: pl.ds(pl.multiple_of(index * PIECE + half * size, size), size)


HALVES = (half_piece(0), half_piece(1))


def slab(index):
    return pl.ds(pl.multiple_of(index * SLICE, SLICE), SLICE)


def gather_col_start(ref, at, send, recv, p, q):
    for i in range(1, D):
        t = lax.rem(q + i, D)
        remote(ref.at[at(q)], ref.at[at(q)], send.at[i], recv.at[q], (p, t)).start()


def gather_col_wait(ref, at, send, recv, p, q):
    for i in range(1, D):
        t = lax.rem(q + i, D)
        remote(ref.at[at(t)], ref.at[at(t)], send.at[i], recv.at[t], (p, t)).wait_recv()


def gather_col_drain(ref, at, send, recv, p, q):
    for i in range(1, D):
        t = lax.rem(q + i, D)
        remote(ref.at[at(q)], ref.at[at(q)], send.at[i], recv.at[q], (p, t)).wait_send()


def gather_row_start(ref, send, recv, p, q, at=None):
    at = at or piece
    for i in range(0, D, 2):
        t = lax.rem(p + i, D) if i else p + 1 - 2 * lax.rem(p, 2)
        remote(ref.at[at(p)], ref.at[at(p)], send.at[i], recv.at[p], (t, q)).start()


def gather_row_pass(ref, send, recv, p, q, number=None, at=None):
    other = p + 1 - 2 * lax.rem(p, 2)
    order = ((2, 14), (4, 12), (6, 10), (8,))
    at = at or piece
    for i in sum(order, ()) if number is None else order[number]:
        t = lax.rem(p + i, D)
        remote(ref.at[at(t)], ref.at[at(t)], send.at[i], recv.at[t], (t, q)).wait_recv()
        remote(ref.at[at(t)], ref.at[at(t)], send.at[i + 1], recv.at[t], (other, q)).start()


def gather_row_wait(ref, send, recv, p, q, at=None):
    other = p + 1 - 2 * lax.rem(p, 2)
    at = at or piece
    for i in range(0, D, 2):
        t = lax.rem(other + i, D)
        remote(ref.at[at(t)], ref.at[at(t)], send.at[i], recv.at[t], (other, q)).wait_recv()


def gather_row_drain(ref, send, recv, p, q, at=None):
    other = p + 1 - 2 * lax.rem(p, 2)
    at = at or piece
    for i in range(0, D, 2):
        remote(ref.at[at(p)], ref.at[at(p)], send.at[i], recv.at[p], (other, q)).wait_send()
        if i:
            t = lax.rem(p + i, D)
            remote(
                ref.at[at(t)], ref.at[at(t)], send.at[i + 1], recv.at[t], (other, q)
            ).wait_send()


TALL, SQUARE, SLABS = (4 * B, B), (B, B), (D, SLICE, B)
PANEL_BUFFERS = dict(
    pr_ref=TALL, pq_ref=TALL, g_ref=SLABS, t_ref=SLABS, tall=TALL, wide=(B, 4 * B), turned=TALL,
    gram=SQUARE, part=SLABS, block=SQUARE, x_ref=TALL, kp_ref=SQUARE, parts=(D, PIECE, B),
    kparts=SLABS, ksum=(SLICE, B), kpair=(SLICE, B), khalf=(SLICE, B), kz=(D // 2, 8, B),
    cp_ref=TALL, cq_ref=TALL, k_ref=SQUARE,
)
PANEL_MANY = (
    "gram_s", "gram_r", "block_s", "gdown_s", "tdown_s", "g_s", "g_r", "t_s", "t_r", "prs_s",
    "pr_s", "pr_r", "pqs_s", "pq_s", "pq_r", "x_s", "x_r", "kp_s", "kp_r", "kz_s", "kz_r",
    "k_s", "k_r", "cp_s", "cp_r", "cq_s", "cq_r",
    "x2_s", "x2_r", "cp2_s", "cp2_r", "cq2_s", "cq2_r",
)
PANEL_ONE = (
    "block_r", "gdown_r", "tdown_r", "prs_r", "pqs_r", "pair_s", "pair_r", "half_s", "half_r",
    "turn_s", "turn_r", "turn2_s", "turn2_r",
)
LOCAL_BUFFERS = dict(
    a_vm=(4 * B, 4 * B), vq_ref=TALL, mid_ref=SQUARE, inv_ref=SQUARE, d_ref=(B // 2, B // 2),
    half_ref=(2, B // 2, B // 2), below_ref=(B // 2, B // 2), w_ref=SQUARE,
)


def tile_rows(tile):
    return pl.ds(pl.multiple_of(tile * B, B), B)


def reduce_kernel(a_ref, a_out, vr_ref, last_high, last_low, *scratch):
    scratch = list(scratch)
    take = lambda names: {name: scratch.pop(0) for name in names}
    local = types.SimpleNamespace(a_ref=a_ref, a_out=a_out, vr_ref=vr_ref, **take(LOCAL_BUFFERS))
    local.last = (last_high, last_low)
    local.turned_vq = (scratch.pop(0), scratch.pop(0))
    local.load, local.store = scratch.pop(0), scratch.pop(0)
    sets = [
        types.SimpleNamespace(**take(PANEL_BUFFERS), **take(PANEL_MANY), **take(PANEL_ONE))
        for _ in range(PANELS)
    ]
    local.loads = [
        pltpu.make_async_copy(
            a_ref.at[pl.ds(0, B)], local.a_vm.at[pl.ds(0, B)], local.load.at[0]
        ),
        pltpu.make_async_copy(
            a_ref.at[pl.ds(B, 3 * B)], local.a_vm.at[pl.ds(B, 3 * B)], local.load.at[1]
        ),
    ]
    for copy in local.loads:
        copy.start()
    greet(lax.axis_index("row"), lax.axis_index("col"))
    local.loads[0].wait()
    drains = [one_panel(panel, local, sets[panel]) for panel in range(PANELS)]
    for drain in drains:
        drain()
    pltpu.make_async_copy(local.a_vm, a_out, local.store).wait()


def subtract(a_vm, left, right, rows):
    a_vm[rows, :] -= dot_split(split(left[rows, :]), (right[0][...], right[1][...]), 1, 0)


def one_panel(panel, local, refs):
    a_vm, vr_ref, vq_ref, mid_ref = local.a_vm, local.vr_ref, local.vq_ref, local.mid_ref
    inv_ref, w_ref = local.inv_ref, local.w_ref
    pr_ref, pq_ref, g_ref, t_ref = refs.pr_ref, refs.pq_ref, refs.g_ref, refs.t_ref
    tall, wide, turned, gram = refs.tall, refs.wide, refs.turned, refs.gram
    part, block, x_ref, kp_ref = refs.part, refs.block, refs.x_ref, refs.kp_ref
    parts, kparts, ksum, kpair = refs.parts, refs.kparts, refs.ksum, refs.kpair
    khalf, kz, cp_ref, cq_ref = refs.khalf, refs.kz, refs.cp_ref, refs.cq_ref
    k_ref, gram_s, gram_r, block_s = refs.k_ref, refs.gram_s, refs.gram_r, refs.block_s
    gdown_s, tdown_s, g_s, g_r = refs.gdown_s, refs.tdown_s, refs.g_s, refs.g_r
    t_s, t_r, prs_s, pr_s = refs.t_s, refs.t_r, refs.prs_s, refs.pr_s
    pr_r, pqs_s, pq_s, pq_r = refs.pr_r, refs.pqs_s, refs.pq_s, refs.pq_r
    kp_s, kp_r = refs.kp_s, refs.kp_r
    kz_s, kz_r, k_s, k_r = refs.kz_s, refs.kz_r, refs.k_s, refs.k_r
    x_sems = ((refs.x_s, refs.x_r), (refs.x2_s, refs.x2_r))
    cp_sems = ((refs.cp_s, refs.cp_r), (refs.cp2_s, refs.cp2_r))
    cq_sems = ((refs.cq_s, refs.cq_r), (refs.cq2_s, refs.cq2_r))
    turn_sems = ((refs.turn_s, refs.turn_r), (refs.turn2_s, refs.turn2_r))
    block_r, gdown_r, tdown_r, prs_r = refs.block_r, refs.gdown_r, refs.tdown_r, refs.prs_r
    pqs_r, pair_s, pair_r, half_s = refs.pqs_r, refs.pair_s, refs.pair_r, refs.half_s
    half_r = refs.half_r
    p, q = lax.axis_index("row"), lax.axis_index("col")
    row_owner, col_owner, top_col = p == panel, q == panel, q == panel + 1
    core = lax.rem(p, 2)
    other = p + 1 - 2 * core
    whole = lambda index: index
    row_peers = [lax.rem(p + i, D) for i in range(D)]
    col_peers = [lax.rem(q + i, D) for i in range(D)]

    @pl.when(row_owner)
    def _():
        wide[...] = a_vm[:B, :]

        @pl.when(q <= panel)
        def _():
            wide[:, :B] = jnp.zeros((B, B), jnp.float32)

        gram[...] = dot(wide[...], wide[...], 1, 1)

    if panel == 0:
        await_greetings(p, q)

    gram_out = lambda i: remote(
        gram.at[slab(col_peers[i])], part.at[q], gram_s.at[i], gram_r.at[q], (p, col_peers[i])
    )
    block_out = lambda i: remote(
        block.at[slab(col_peers[i])], t_ref.at[col_peers[i]], block_s.at[i], block_r,
        (p, col_peers[i]),
    )
    pq_out = lambda i: remote(
        turned.at[piece(row_peers[i])], pq_ref.at[piece(row_peers[i])], pqs_s.at[i], pqs_r,
        (row_peers[i], q),
    )
    pr_out = lambda i: remote(
        tall.at[piece(col_peers[i])], pr_ref.at[piece(col_peers[i])], prs_s.at[i], prs_r,
        (p, col_peers[i]),
    )
    g_down = lambda i: remote(
        g_ref.at[q], g_ref.at[q], gdown_s.at[i], gdown_r, (row_peers[i], q)
    )
    t_down = lambda i: remote(
        t_ref.at[q], t_ref.at[q], tdown_s.at[i], tdown_r, (row_peers[i], q)
    )

    @pl.when(row_owner)
    def _():
        for i in range(1, D):
            gram_out(i).start()
        part[q] = gram[slab(q), :]

        @pl.when(top_col)
        def _():
            block[...] = wide[:, :B].T
            for i in range(1, D):
                block_out(i).start()
            t_ref[q] = block[slab(q), :]

        turned[...] = wide[...].T
        for i in range(1, D):
            pq_out(i).start()
        pq_ref[piece(p), :] = turned[piece(p), :]

    if panel == 0:
        local.loads[1].wait()
    else:
        for tile in range(1, 4):
            subtract(a_vm, vr_ref, local.last, slice(tile * B, tile * B + B))

    @pl.when(col_owner)
    def _():
        tall[...] = a_vm[:, :B]

        @pl.when(p <= panel)
        def _():
            tall[:B, :] = jnp.zeros((B, B), jnp.float32)

        for i in range(1, D):
            pr_out(i).start()
        pr_ref[piece(q), :] = tall[piece(q), :]

    @pl.when(row_owner)
    def _():
        for i in range(1, D):
            t = col_peers[i]
            remote(gram.at[slab(q)], part.at[t], gram_s.at[i], gram_r.at[t], (p, t)).wait_recv()
        total = part[0]
        for i in range(1, D):
            total = total + part[i]
        g_ref[q] = total
        for i in range(1, D):
            g_down(i).start()

        @pl.when(jnp.logical_not(top_col))
        def _():
            block_out(1).wait_recv()

        for i in range(1, D):
            t_down(i).start()

    @pl.when(jnp.logical_not(row_owner))
    def _():
        g_down(1).wait_recv()

    gather_col_start(g_ref, whole, g_s, g_r, p, q)

    @pl.when(jnp.logical_not(row_owner))
    def _():
        t_down(1).wait_recv()

    gather_col_start(t_ref, whole, t_s, t_r, p, q)

    @pl.when(jnp.logical_not(row_owner))
    def _():
        pq_out(1).wait_recv()

    gather_row_start(pq_ref, pq_s, pq_r, p, q)

    gather_col_wait(g_ref, whole, g_s, g_r, p, q)

    @pl.when(jnp.logical_not(col_owner))
    def _():
        pr_out(1).wait_recv()

    gather_col_start(pr_ref, piece, pr_s, pr_r, p, q)

    kp_ref[...] = g_ref[...].reshape(B, B)
    chol_inverse(kp_ref, inv_ref, local.d_ref, local.half_ref, local.below_ref)
    gather_row_pass(pq_ref, pq_s, pq_r, p, q)
    gather_col_wait(t_ref, whole, t_s, t_r, p, q)
    inverse_low = inv_ref[...]
    top = dot(t_ref[...].reshape(B, B), inverse_low, 1, 1)
    w_ref[...] = top

    def polar_step(i, carry):
        w = w_ref[...]
        s = split(w)
        w_ref[...] = 1.5 * w - 0.5 * dot_split(split(dot_split(s, s, 1, 1)), s, 1, 0)
        return carry

    lax.fori_loop(0, NS_STEPS, polar_step, 0)
    w = w_ref[...]
    w_split = split(w)
    cross = dot_split(w_split, split(top), 0, 0)
    metric = eye() + cross + cross.T + dot_split(w_split, w_split, 0, 0)
    guess = (40.0 / 41.0) * eye() - (8.0 / 41.0) * metric
    for i in range(4):
        guess = guess + dot3(guess, eye() - dot3(metric, guess, 1, 0), 1, 0)
    mid_ref[...] = 2.0 * guess

    gather_row_wait(pq_ref, pq_s, pq_r, p, q)
    inv_split = split(inverse_low)

    def reflect(ref, out):
        def step(tile, carry):
            rows = pl.ds(pl.multiple_of(tile * B, B), B)
            out[rows, :] = dot_split(split(ref[rows, :]), inv_split, 1, 1)
            return carry

        lax.fori_loop(0, 4, step, 0)

    reflect(pq_ref, vq_ref)

    @pl.when(top_col)
    def _():
        vq_ref[:B, :] = vq_ref[:B, :] + w

    vq = split(vq_ref[...])
    inner = [slice(0, PIECE // 2), slice(PIECE // 2, PIECE)]
    within = [pl.ds(0, PIECE // 2), pl.ds(PIECE // 2, PIECE // 2)]

    def x_out(t, h):
        send, recv = x_sems[h]
        return remote(
            x_ref.at[HALVES[h](t)], parts.at[q, within[h]], send.at[t], recv.at[q], (p, t)
        )

    def product_step(number, carry):
        tile = lax.rem(q // 4 + number, 4)
        rows = pl.ds(pl.multiple_of(tile * B, B), B)
        x = dot_split(split(a_vm[rows, :]), vq, 1, 0)
        x_ref[rows, :] = x
        for i in range(4):
            t = 4 * tile + lax.rem(q + i, 4)

            @pl.when(t != q)
            def _():
                x_out(t, 0).start()

        return carry

    lax.fori_loop(0, 4, product_step, 0)
    for i in range(1, D):
        x_out(col_peers[i], 1).start()

    gather_col_wait(pr_ref, piece, pr_s, pr_r, p, q)
    reflect(pr_ref, vr_ref)

    @pl.when(p == panel + 1)
    def _():
        vr_ref[:B, :] = vr_ref[:B, :] + w_ref[...]

    kp_ref[...] = dot3(vr_ref[...], x_ref[...], 0, 0)
    parts[q] = x_ref[piece(q), :]
    kp_out = lambda i: remote(
        kp_ref.at[slab(col_peers[i])], kparts.at[q], kp_s.at[i], kp_r.at[q], (p, col_peers[i])
    )
    for i in range(1, D):
        kp_out(i).start()
    kparts[q] = kp_ref[slab(q), :]

    for tile in range(4):
        rows = slice(tile * B, tile * B + B)
        local.turned_vq[0][:, rows], local.turned_vq[1][:, rows] = split(vq_ref[rows, :].T)

    def turn_out(h):
        send, recv = turn_sems[h]
        return remote(cp_ref.at[HALVES[h](q)], cq_ref.at[HALVES[h](q)], send, recv, (q, p))

    def turn_in(h):
        send, recv = turn_sems[h]

        @pl.when(p != q)
        def _():
            remote(
                cp_ref.at[HALVES[h](q)], cq_ref.at[HALVES[h](p)], send, recv, (q, p)
            ).wait_recv()

        gather_row_start(cq_ref, *cq_sems[h], p, q, at=HALVES[h])

    def image_half(h):
        send, recv = x_sems[h]
        for i in range(1, D):
            t = col_peers[i]
            remote(
                x_ref.at[HALVES[h](q)], parts.at[t, within[h]], send.at[t], recv.at[t], (p, t)
            ).wait_recv()
        total = parts[0, inner[h]]
        for i in range(1, D):
            total = total + parts[i, inner[h]]
        image = dot(total, mid_ref[...], 1, 0)
        cp_ref[HALVES[h](q), :] = image

        @pl.when(p != q)
        def _():
            turn_out(h).start()

        @pl.when(p == q)
        def _():
            cq_ref[HALVES[h](p), :] = image

        gather_col_start(cp_ref, HALVES[h], *cp_sems[h], p, q)

    image_half(0)
    image_half(1)
    turn_in(0)

    for i in range(1, D):
        t = col_peers[i]
        remote(kp_ref.at[slab(q)], kparts.at[t], kp_s.at[i], kp_r.at[t], (p, t)).wait_recv()
    total = kparts[0]
    for i in range(1, D):
        total = total + kparts[i]
    ksum[...] = total
    pair_out = remote(ksum, kpair, pair_s, pair_r, (other, q))
    pair_out.start()
    pair_out.wait_recv()
    khalf[...] = ksum[...] + kpair[...]
    mine = pl.ds(pl.multiple_of(core * 8, 8), 8)
    kz_out = lambda i: remote(
        khalf.at[mine], kz.at[p // 2], kz_s.at[i // 2], kz_r.at[p // 2], (row_peers[i], q)
    )
    for i in range(2, D, 2):
        kz_out(i).start()
    kz[p // 2] = khalf[mine, :]

    turn_in(1)
    for i in range(2, D, 2):
        t = row_peers[i] // 2
        remote(
            khalf.at[mine], kz.at[t], kz_s.at[i // 2], kz_r.at[t], (row_peers[i], q)
        ).wait_recv()
    total = kz[0]
    for i in range(1, D // 2):
        total = total + kz[i]
    here = pl.ds(pl.multiple_of(q * SLICE + core * 8, 8), 8)
    there = pl.ds(pl.multiple_of(q * SLICE + 8 - core * 8, 8), 8)
    k_ref[here, :] = total
    half_out = remote(k_ref.at[here], k_ref.at[here], half_s, half_r, (other, q))
    half_out.start()
    remote(k_ref.at[there], k_ref.at[there], half_s, half_r, (other, q)).wait_recv()
    gather_col_start(k_ref, slab, k_s, k_r, p, q)
    for number in range(4):
        tile = lax.rem(q // 4 + number, 4)
        for i in range(4):
            t = 4 * tile + lax.rem(q + i, 4)

            @pl.when(t != q)
            def _():
                for at, (send, recv) in zip(HALVES, cp_sems):
                    remote(
                        cp_ref.at[at(t)], cp_ref.at[at(t)], send.at[0], recv.at[t], (p, t)
                    ).wait_recv()

        subtract(a_vm, cp_ref, local.turned_vq, tile_rows(tile))
        for at, sems in zip(HALVES, cq_sems):
            gather_row_pass(cq_ref, *sems, p, q, number, at=at)
    if panel == PANELS - 1:
        pltpu.make_async_copy(a_vm, local.a_out, local.store).start()
    gather_col_wait(k_ref, slab, k_s, k_r, p, q)
    middle = mid_ref[...]
    shift = dot3(dot3(middle, k_ref[...], 1, 0), middle, 1, 0)
    shift = split(0.5 * (shift + shift.T))
    for at, sems in zip(HALVES, cq_sems):
        gather_row_wait(cq_ref, *sems, p, q, at=at)
    for tile in range(4):
        rows = slice(tile * B, tile * B + B)
        rest = cq_ref[rows, :] - dot_split(split(vq_ref[rows, :]), shift, 1, 0)
        local.last[0][:, rows], local.last[1][:, rows] = split(rest.T)
    if panel < PANELS - 1:
        subtract(a_vm, vr_ref, local.last, slice(0, B))

    def drain():
        for h in range(2):
            gather_row_drain(cq_ref, *cq_sems[h], p, q, at=HALVES[h])
            gather_col_drain(cp_ref, HALVES[h], *cp_sems[h], p, q)
        gather_row_drain(pq_ref, pq_s, pq_r, p, q)
        for ref, at, send, recv in (
            (k_ref, slab, k_s, k_r), (pr_ref, piece, pr_s, pr_r),
            (g_ref, whole, g_s, g_r), (t_ref, whole, t_s, t_r),
        ):
            gather_col_drain(ref, at, send, recv, p, q)

        @pl.when(p != q)
        def _():
            turn_out(0).wait_send()
            turn_out(1).wait_send()

        pair_out.wait_send()
        half_out.wait_send()
        for i in range(2, D, 2):
            kz_out(i).wait_send()
        for i in range(1, D):
            kp_out(i).wait_send()
            x_out(col_peers[i], 0).wait_send()
            x_out(col_peers[i], 1).wait_send()

        @pl.when(row_owner)
        def _():
            for i in range(1, D):
                gram_out(i).wait_send()
                pq_out(i).wait_send()
                g_down(i).wait_send()
                t_down(i).wait_send()

            @pl.when(top_col)
            def _():
                for i in range(1, D):
                    block_out(i).wait_send()

        @pl.when(col_owner)
        def _():
            for i in range(1, D):
                pr_out(i).wait_send()

    return drain


def reduce_panels(matrix):
    vmem, anywhere = pl.BlockSpec(memory_space=pltpu.VMEM), pl.BlockSpec(memory_space=pl.ANY)
    buffers = lambda shapes: [pltpu.VMEM(shape, jnp.float32) for shape in shapes.values()]
    many, one = pltpu.SemaphoreType.DMA((D,)), pltpu.SemaphoreType.DMA
    right = jax.ShapeDtypeStruct((B, 4 * B), jnp.bfloat16)
    panel_set = buffers(PANEL_BUFFERS) + [many] * len(PANEL_MANY) + [one] * len(PANEL_ONE)
    return pl.pallas_call(
        reduce_kernel,
        out_shape=(
            jax.ShapeDtypeStruct((4 * B, 4 * B), jnp.float32),
            jax.ShapeDtypeStruct(TALL, jnp.float32), right, right,
        ),
        in_specs=[anywhere],
        out_specs=(anywhere, vmem, vmem, vmem),
        scratch_shapes=buffers(LOCAL_BUFFERS)
        + [pltpu.VMEM((B, 4 * B), jnp.bfloat16)] * 2
        + [pltpu.SemaphoreType.DMA((2,)), one]
        + panel_set * PANELS,
        compiler_params=pltpu.CompilerParams(
            collective_id=1, has_side_effects=True, vmem_limit_bytes=VMEM_LIMIT
        ),
        name="reduce_panels",
    )(matrix)


def finish_kernel(a_ref, vr_ref, high_ref, low_ref, out_ref):
    out_ref[...] = a_ref[...] - dot_split(
        split(vr_ref[...]), (high_ref[...], low_ref[...]), 1, 0
    )


def finish(matrix, vr, high, low):
    rows, size = B, 4 * B
    tile = lambda width: pl.BlockSpec((rows, width), lambda i: (i, 0))
    whole = pl.BlockSpec((B, size), lambda i: (0, 0))
    return pl.pallas_call(
        finish_kernel,
        out_shape=jax.ShapeDtypeStruct((size, size), jnp.float32),
        grid=(size // rows,),
        in_specs=[tile(size), tile(B), whole, whole],
        out_specs=tile(size),
        compiler_params=pltpu.CompilerParams(vmem_limit_bytes=VMEM_LIMIT),
        name="finish",
    )(matrix, vr, high, low)


def body(affinity):
    return finish(*reduce_panels(affinity))


def solution(mesh):
    return jax.shard_map(
        body,
        mesh=mesh,
        in_specs=(P("row", "col"),),
        out_specs=P("row", "col"),
        check_vma=False,
    )
```

```python
import types

import jax
import jax.numpy as jnp
from jax import lax
from jax.experimental import pallas as pl
from jax.experimental.pallas import tpu as pltpu
from jax.sharding import PartitionSpec as P

B = 256
PANELS = 2
NS_STEPS = 12
D = 16
PIECE = 64
SLICE = 16
MESH = pl.DeviceIdType.MESH
HIGHEST = lax.Precision.HIGHEST
VMEM_LIMIT = 56 * 1024 * 1024


def dot(first, second, first_dim, second_dim):
    return lax.dot_general(
        first,
        second,
        (((first_dim,), (second_dim,)), ((), ())),
        precision=HIGHEST,
        preferred_element_type=jnp.float32,
    )


def split(value):
    high = value.astype(jnp.bfloat16)
    return high, (value - high.astype(jnp.float32)).astype(jnp.bfloat16)


def dot_split(first, second, first_dim, second_dim):
    def one(x, y):
        return lax.dot_general(
            x, y, (((first_dim,), (second_dim,)), ((), ())), preferred_element_type=jnp.float32
        )

    return one(first[0], second[0]) + (one(first[0], second[1]) + one(first[1], second[0]))


def dot3(first, second, first_dim, second_dim):
    return dot_split(split(first), split(second), first_dim, second_dim)


def sublane(x, j):
    return jnp.broadcast_to(x[j : j + 1, :], x.shape)


def chol_inverse_128(d_ref):
    n = 128
    sub = lax.broadcasted_iota(jnp.int32, (8, n), 0)
    lane = lax.broadcasted_iota(jnp.int32, (8, n), 1)
    rows = [d_ref[8 * g : 8 * g + 8, :] for g in range(n // 8)]
    for g in range(n // 8):
        k0 = 8 * g
        own = (lane >= k0) & (lane < k0 + 8)
        unit = jnp.where(lane == sub + k0, 1.0, 0.0)
        cur = rows[g]
        cols = [jnp.broadcast_to(cur[:, k0 + j : k0 + j + 1], (8, n)) for j in range(8)]
        cur = jnp.where(own, unit, cur)
        recips, factors, pivots = [], {}, []
        diag = jnp.ones((8, n), jnp.float32)
        for j in range(8):
            d = sublane(cols[j], j)
            recips.append(1.0 / d)
            diag = jnp.where(sub == j, d, diag)
            f = cols[j] * recips[j]
            for l in range(j + 1, 8):
                factors[j, l] = sublane(cols[l], j)
                cols[l] = cols[l] - f * factors[j, l]
            pivots.append(sublane(cur, j))
            cur = cur - jnp.where(sub > j, f, 0.0) * pivots[j]
        d_ref[k0 : k0 + 8, :] = jnp.where(lane < k0 + 8, cur, 0.0) / jnp.sqrt(diag)
        for i in range(g + 1, n // 8):
            low = rows[i]
            cols = [jnp.broadcast_to(low[:, k0 + j : k0 + j + 1], (8, n)) for j in range(8)]
            low = jnp.where(own, 0.0, low)
            for j in range(8):
                f = cols[j] * recips[j]
                for l in range(j + 1, 8):
                    cols[l] = cols[l] - f * factors[j, l]
                low = low - f * pivots[j]
            rows[i] = low


def chol_inverse(gram_ref, out_ref, d_ref, half_ref, below_ref):
    half = B // 2
    d_ref[...] = gram_ref[:half, :half]

    def step(i, carry):
        chol_inverse_128(d_ref)
        half_ref[i] = d_ref[...]

        @pl.when(i == 0)
        def _():
            below = dot(gram_ref[half:, :half], d_ref[...], 1, 1)
            below_ref[...] = below
            d_ref[...] = gram_ref[half:, half:] - dot(below, below, 1, 1)

        return carry

    lax.fori_loop(0, 2, step, 0)
    first, second = half_ref[0], half_ref[1]
    out_ref[:half, :half] = first
    out_ref[:half, half:] = jnp.zeros((half, half), jnp.float32)
    out_ref[half:, :half] = -dot(second, dot(below_ref[...], first, 1, 0), 1, 0)
    out_ref[half:, half:] = second


def eye():
    r = lax.broadcasted_iota(jnp.int32, (B, B), 0)
    c = lax.broadcasted_iota(jnp.int32, (B, B), 1)
    return jnp.where(r == c, 1.0, 0.0)


def greet(p, q):
    barrier = pltpu.get_barrier_semaphore()
    for i in range(1, D):
        pl.semaphore_signal(
            barrier, inc=1, device_id=(lax.rem(p + i, D), q), device_id_type=MESH
        )
        pl.semaphore_signal(
            barrier, inc=1, device_id=(p, lax.rem(q + i, D)), device_id_type=MESH
        )

    @pl.when(p != q)
    def _():
        pl.semaphore_signal(barrier, inc=1, device_id=(q, p), device_id_type=MESH)


def await_greetings(p, q):
    barrier = pltpu.get_barrier_semaphore()

    @pl.when(p != q)
    def _():
        pl.semaphore_wait(barrier, 2 * (D - 1) + 1)

    @pl.when(p == q)
    def _():
        pl.semaphore_wait(barrier, 2 * (D - 1))


def remote(src, dst, send, recv, target):
    return pltpu.make_async_remote_copy(
        src_ref=src, dst_ref=dst, send_sem=send, recv_sem=recv,
        device_id=target, device_id_type=MESH,
    )


def piece(index):
    return pl.ds(pl.multiple_of(index * PIECE, PIECE), PIECE)


def half_piece(half):
    size = PIECE // 2
    return lambda index: pl.ds(pl.multiple_of(index * PIECE + half * size, size), size)


HALVES = (half_piece(0), half_piece(1))


def slab(index):
    return pl.ds(pl.multiple_of(index * SLICE, SLICE), SLICE)


def gather_col_start(ref, at, send, recv, p, q):
    for i in range(1, D):
        t = lax.rem(q + i, D)
        remote(ref.at[at(q)], ref.at[at(q)], send.at[i], recv.at[q], (p, t)).start()


def gather_col_wait(ref, at, send, recv, p, q):
    for i in range(1, D):
        t = lax.rem(q + i, D)
        remote(ref.at[at(t)], ref.at[at(t)], send.at[i], recv.at[t], (p, t)).wait_recv()


def gather_col_drain(ref, at, send, recv, p, q):
    for i in range(1, D):
        t = lax.rem(q + i, D)
        remote(ref.at[at(q)], ref.at[at(q)], send.at[i], recv.at[q], (p, t)).wait_send()


def gather_row_start(ref, send, recv, p, q, at=None):
    at = at or piece
    for i in range(0, D, 2):
        t = lax.rem(p + i, D) if i else p + 1 - 2 * lax.rem(p, 2)
        remote(ref.at[at(p)], ref.at[at(p)], send.at[i], recv.at[p], (t, q)).start()


def gather_row_pass(ref, send, recv, p, q, number=None, at=None):
    other = p + 1 - 2 * lax.rem(p, 2)
    order = ((2, 14), (4, 12), (6, 10), (8,))
    at = at or piece
    for i in sum(order, ()) if number is None else order[number]:
        t = lax.rem(p + i, D)
        remote(ref.at[at(t)], ref.at[at(t)], send.at[i], recv.at[t], (t, q)).wait_recv()
        remote(ref.at[at(t)], ref.at[at(t)], send.at[i + 1], recv.at[t], (other, q)).start()


def gather_row_wait(ref, send, recv, p, q, at=None):
    other = p + 1 - 2 * lax.rem(p, 2)
    at = at or piece
    for i in range(0, D, 2):
        t = lax.rem(other + i, D)
        remote(ref.at[at(t)], ref.at[at(t)], send.at[i], recv.at[t], (other, q)).wait_recv()


def gather_row_drain(ref, send, recv, p, q, at=None):
    other = p + 1 - 2 * lax.rem(p, 2)
    at = at or piece
    for i in range(0, D, 2):
        remote(ref.at[at(p)], ref.at[at(p)], send.at[i], recv.at[p], (other, q)).wait_send()
        if i:
            t = lax.rem(p + i, D)
            remote(
                ref.at[at(t)], ref.at[at(t)], send.at[i + 1], recv.at[t], (other, q)
            ).wait_send()


TALL, SQUARE, SLABS = (4 * B, B), (B, B), (D, SLICE, B)
PANEL_BUFFERS = dict(
    pr_ref=TALL, pq_ref=TALL, g_ref=SLABS, t_ref=SLABS, tall=TALL, wide=(B, 4 * B), turned=TALL,
    gram=SQUARE, part=SLABS, block=SQUARE, x_ref=TALL, kp_ref=SQUARE, parts=(D, PIECE, B),
    kparts=SLABS, ksum=(SLICE, B), kpair=(SLICE, B), khalf=(SLICE, B), kz=(D // 2, 8, B),
    cp_ref=TALL, cq_ref=TALL, k_ref=SQUARE,
)
PANEL_MANY = (
    "gram_s", "gram_r", "block_s", "gdown_s", "tdown_s", "g_s", "g_r", "t_s", "t_r", "prs_s",
    "pr_s", "pr_r", "pqs_s", "pq_s", "pq_r", "x_s", "x_r", "kp_s", "kp_r", "kz_s", "kz_r",
    "k_s", "k_r", "cp_s", "cp_r", "cq_s", "cq_r",
    "x2_s", "x2_r", "cp2_s", "cp2_r", "cq2_s", "cq2_r",
)
PANEL_ONE = (
    "block_r", "gdown_r", "tdown_r", "prs_r", "pqs_r", "pair_s", "pair_r", "half_s", "half_r",
    "turn_s", "turn_r", "turn2_s", "turn2_r",
)
LOCAL_BUFFERS = dict(
    a_vm=(4 * B, 4 * B), vq_ref=TALL, mid_ref=SQUARE, inv_ref=SQUARE, d_ref=(B // 2, B // 2),
    half_ref=(2, B // 2, B // 2), below_ref=(B // 2, B // 2), w_ref=SQUARE,
)


def tile_rows(tile):
    return pl.ds(pl.multiple_of(tile * B, B), B)


def reduce_kernel(a_ref, a_out, vr_ref, last_high, last_low, *scratch):
    scratch = list(scratch)
    take = lambda names: {name: scratch.pop(0) for name in names}
    local = types.SimpleNamespace(a_ref=a_ref, a_out=a_out, vr_ref=vr_ref, **take(LOCAL_BUFFERS))
    local.last = (last_high, last_low)
    local.turned_vq = (scratch.pop(0), scratch.pop(0))
    local.load, local.store = scratch.pop(0), scratch.pop(0)
    sets = [
        types.SimpleNamespace(**take(PANEL_BUFFERS), **take(PANEL_MANY), **take(PANEL_ONE))
        for _ in range(PANELS)
    ]
    local.loads = [
        pltpu.make_async_copy(
            a_ref.at[pl.ds(0, B)], local.a_vm.at[pl.ds(0, B)], local.load.at[0]
        ),
        pltpu.make_async_copy(
            a_ref.at[pl.ds(B, 3 * B)], local.a_vm.at[pl.ds(B, 3 * B)], local.load.at[1]
        ),
    ]
    for copy in local.loads:
        copy.start()
    greet(lax.axis_index("row"), lax.axis_index("col"))
    local.loads[0].wait()
    drains = [one_panel(panel, local, sets[panel]) for panel in range(PANELS)]
    for drain in drains:
        drain()
    pltpu.make_async_copy(local.a_vm, a_out, local.store).wait()


def subtract(a_vm, left, right, rows):
    a_vm[rows, :] -= dot_split(split(left[rows, :]), (right[0][...], right[1][...]), 1, 0)


def one_panel(panel, local, refs):
    a_vm, vr_ref, vq_ref, mid_ref = local.a_vm, local.vr_ref, local.vq_ref, local.mid_ref
    inv_ref, w_ref = local.inv_ref, local.w_ref
    pr_ref, pq_ref, g_ref, t_ref = refs.pr_ref, refs.pq_ref, refs.g_ref, refs.t_ref
    tall, wide, turned, gram = refs.tall, refs.wide, refs.turned, refs.gram
    part, block, x_ref, kp_ref = refs.part, refs.block, refs.x_ref, refs.kp_ref
    parts, kparts, ksum, kpair = refs.parts, refs.kparts, refs.ksum, refs.kpair
    khalf, kz, cp_ref, cq_ref = refs.khalf, refs.kz, refs.cp_ref, refs.cq_ref
    k_ref, gram_s, gram_r, block_s = refs.k_ref, refs.gram_s, refs.gram_r, refs.block_s
    gdown_s, tdown_s, g_s, g_r = refs.gdown_s, refs.tdown_s, refs.g_s, refs.g_r
    t_s, t_r, prs_s, pr_s = refs.t_s, refs.t_r, refs.prs_s, refs.pr_s
    pr_r, pqs_s, pq_s, pq_r = refs.pr_r, refs.pqs_s, refs.pq_s, refs.pq_r
    kp_s, kp_r = refs.kp_s, refs.kp_r
    kz_s, kz_r, k_s, k_r = refs.kz_s, refs.kz_r, refs.k_s, refs.k_r
    x_sems = ((refs.x_s, refs.x_r), (refs.x2_s, refs.x2_r))
    cp_sems = ((refs.cp_s, refs.cp_r), (refs.cp2_s, refs.cp2_r))
    cq_sems = ((refs.cq_s, refs.cq_r), (refs.cq2_s, refs.cq2_r))
    turn_sems = ((refs.turn_s, refs.turn_r), (refs.turn2_s, refs.turn2_r))
    block_r, gdown_r, tdown_r, prs_r = refs.block_r, refs.gdown_r, refs.tdown_r, refs.prs_r
    pqs_r, pair_s, pair_r, half_s = refs.pqs_r, refs.pair_s, refs.pair_r, refs.half_s
    half_r = refs.half_r
    p, q = lax.axis_index("row"), lax.axis_index("col")
    row_owner, col_owner, top_col = p == panel, q == panel, q == panel + 1
    core = lax.rem(p, 2)
    other = p + 1 - 2 * core
    whole = lambda index: index
    row_peers = [lax.rem(p + i, D) for i in range(D)]
    col_peers = [lax.rem(q + i, D) for i in range(D)]

    @pl.when(row_owner)
    def _():
        wide[...] = a_vm[:B, :]

        @pl.when(q <= panel)
        def _():
            wide[:, :B] = jnp.zeros((B, B), jnp.float32)

        gram[...] = dot(wide[...], wide[...], 1, 1)

    if panel == 0:
        await_greetings(p, q)

    gram_out = lambda i: remote(
        gram.at[slab(col_peers[i])], part.at[q], gram_s.at[i], gram_r.at[q], (p, col_peers[i])
    )
    block_out = lambda i: remote(
        block.at[slab(col_peers[i])], t_ref.at[col_peers[i]], block_s.at[i], block_r,
        (p, col_peers[i]),
    )
    pq_out = lambda i: remote(
        turned.at[piece(row_peers[i])], pq_ref.at[piece(row_peers[i])], pqs_s.at[i], pqs_r,
        (row_peers[i], q),
    )
    pr_out = lambda i: remote(
        tall.at[piece(col_peers[i])], pr_ref.at[piece(col_peers[i])], prs_s.at[i], prs_r,
        (p, col_peers[i]),
    )
    g_down = lambda i: remote(
        g_ref.at[q], g_ref.at[q], gdown_s.at[i], gdown_r, (row_peers[i], q)
    )
    t_down = lambda i: remote(
        t_ref.at[q], t_ref.at[q], tdown_s.at[i], tdown_r, (row_peers[i], q)
    )

    @pl.when(row_owner)
    def _():
        for i in range(1, D):
            gram_out(i).start()
        part[q] = gram[slab(q), :]

        @pl.when(top_col)
        def _():
            block[...] = wide[:, :B].T
            for i in range(1, D):
                block_out(i).start()
            t_ref[q] = block[slab(q), :]

        turned[...] = wide[...].T
        for i in range(1, D):
            pq_out(i).start()
        pq_ref[piece(p), :] = turned[piece(p), :]

    if panel == 0:
        local.loads[1].wait()
    else:
        for tile in range(1, 4):
            subtract(a_vm, vr_ref, local.last, slice(tile * B, tile * B + B))

    @pl.when(col_owner)
    def _():
        tall[...] = a_vm[:, :B]

        @pl.when(p <= panel)
        def _():
            tall[:B, :] = jnp.zeros((B, B), jnp.float32)

        for i in range(1, D):
            pr_out(i).start()
        pr_ref[piece(q), :] = tall[piece(q), :]

    @pl.when(row_owner)
    def _():
        for i in range(1, D):
            t = col_peers[i]
            remote(gram.at[slab(q)], part.at[t], gram_s.at[i], gram_r.at[t], (p, t)).wait_recv()
        total = part[0]
        for i in range(1, D):
            total = total + part[i]
        g_ref[q] = total
        for i in range(1, D):
            g_down(i).start()

        @pl.when(jnp.logical_not(top_col))
        def _():
            block_out(1).wait_recv()

        for i in range(1, D):
            t_down(i).start()

    @pl.when(jnp.logical_not(row_owner))
    def _():
        g_down(1).wait_recv()

    gather_col_start(g_ref, whole, g_s, g_r, p, q)

    @pl.when(jnp.logical_not(row_owner))
    def _():
        t_down(1).wait_recv()

    gather_col_start(t_ref, whole, t_s, t_r, p, q)

    @pl.when(jnp.logical_not(row_owner))
    def _():
        pq_out(1).wait_recv()

    gather_row_start(pq_ref, pq_s, pq_r, p, q)

    gather_col_wait(g_ref, whole, g_s, g_r, p, q)

    @pl.when(jnp.logical_not(col_owner))
    def _():
        pr_out(1).wait_recv()

    gather_col_start(pr_ref, piece, pr_s, pr_r, p, q)

    kp_ref[...] = g_ref[...].reshape(B, B)
    chol_inverse(kp_ref, inv_ref, local.d_ref, local.half_ref, local.below_ref)
    gather_row_pass(pq_ref, pq_s, pq_r, p, q)
    gather_col_wait(t_ref, whole, t_s, t_r, p, q)
    inverse_low = inv_ref[...]
    top = dot(t_ref[...].reshape(B, B), inverse_low, 1, 1)
    w_ref[...] = top

    def polar_step(i, carry):
        w = w_ref[...]
        s = split(w)
        w_ref[...] = 1.5 * w - 0.5 * dot_split(split(dot_split(s, s, 1, 1)), s, 1, 0)
        return carry

    lax.fori_loop(0, NS_STEPS, polar_step, 0)
    w = w_ref[...]
    w_split = split(w)
    cross = dot_split(w_split, split(top), 0, 0)
    metric = eye() + cross + cross.T + dot_split(w_split, w_split, 0, 0)
    guess = (40.0 / 41.0) * eye() - (8.0 / 41.0) * metric
    for i in range(4):
        guess = guess + dot3(guess, eye() - dot3(metric, guess, 1, 0), 1, 0)
    mid_ref[...] = 2.0 * guess

    gather_row_wait(pq_ref, pq_s, pq_r, p, q)
    inv_split = split(inverse_low)

    def reflect(ref, out):
        def step(tile, carry):
            rows = pl.ds(pl.multiple_of(tile * B, B), B)
            out[rows, :] = dot_split(split(ref[rows, :]), inv_split, 1, 1)
            return carry

        lax.fori_loop(0, 4, step, 0)

    reflect(pq_ref, vq_ref)

    @pl.when(top_col)
    def _():
        vq_ref[:B, :] = vq_ref[:B, :] + w

    vq = split(vq_ref[...])
    inner = [slice(0, PIECE // 2), slice(PIECE // 2, PIECE)]
    within = [pl.ds(0, PIECE // 2), pl.ds(PIECE // 2, PIECE // 2)]

    def x_out(t, h):
        send, recv = x_sems[h]
        return remote(
            x_ref.at[HALVES[h](t)], parts.at[q, within[h]], send.at[t], recv.at[q], (p, t)
        )

    def product_step(number, carry):
        tile = lax.rem(q // 4 + number, 4)
        rows = pl.ds(pl.multiple_of(tile * B, B), B)
        x = dot_split(split(a_vm[rows, :]), vq, 1, 0)
        x_ref[rows, :] = x
        for i in range(4):
            t = 4 * tile + lax.rem(q + i, 4)

            @pl.when(t != q)
            def _():
                x_out(t, 0).start()

        return carry

    lax.fori_loop(0, 4, product_step, 0)
    for i in range(1, D):
        x_out(col_peers[i], 1).start()

    gather_col_wait(pr_ref, piece, pr_s, pr_r, p, q)
    reflect(pr_ref, vr_ref)

    @pl.when(p == panel + 1)
    def _():
        vr_ref[:B, :] = vr_ref[:B, :] + w_ref[...]

    kp_ref[...] = dot3(vr_ref[...], x_ref[...], 0, 0)
    parts[q] = x_ref[piece(q), :]
    kp_out = lambda i: remote(
        kp_ref.at[slab(col_peers[i])], kparts.at[q], kp_s.at[i], kp_r.at[q], (p, col_peers[i])
    )
    for i in range(1, D):
        kp_out(i).start()
    kparts[q] = kp_ref[slab(q), :]

    for tile in range(4):
        rows = slice(tile * B, tile * B + B)
        local.turned_vq[0][:, rows], local.turned_vq[1][:, rows] = split(vq_ref[rows, :].T)

    def turn_out(h):
        send, recv = turn_sems[h]
        return remote(cp_ref.at[HALVES[h](q)], cq_ref.at[HALVES[h](q)], send, recv, (q, p))

    def turn_in(h):
        send, recv = turn_sems[h]

        @pl.when(p != q)
        def _():
            remote(
                cp_ref.at[HALVES[h](q)], cq_ref.at[HALVES[h](p)], send, recv, (q, p)
            ).wait_recv()

        gather_row_start(cq_ref, *cq_sems[h], p, q, at=HALVES[h])

    middle_split = split(mid_ref[...])

    def image_half(h):
        send, recv = x_sems[h]
        for i in range(1, D):
            t = col_peers[i]
            remote(
                x_ref.at[HALVES[h](q)], parts.at[t, within[h]], send.at[t], recv.at[t], (p, t)
            ).wait_recv()
        total = parts[0, inner[h]]
        for i in range(1, D):
            total = total + parts[i, inner[h]]
        image = dot_split(split(total), middle_split, 1, 0)
        cp_ref[HALVES[h](q), :] = image

        @pl.when(p != q)
        def _():
            turn_out(h).start()

        @pl.when(p == q)
        def _():
            cq_ref[HALVES[h](p), :] = image

        gather_col_start(cp_ref, HALVES[h], *cp_sems[h], p, q)

    image_half(0)
    image_half(1)
    turn_in(0)

    for i in range(1, D):
        t = col_peers[i]
        remote(kp_ref.at[slab(q)], kparts.at[t], kp_s.at[i], kp_r.at[t], (p, t)).wait_recv()
    total = kparts[0]
    for i in range(1, D):
        total = total + kparts[i]
    ksum[...] = total
    pair_out = remote(ksum, kpair, pair_s, pair_r, (other, q))
    pair_out.start()
    pair_out.wait_recv()
    khalf[...] = ksum[...] + kpair[...]
    mine = pl.ds(pl.multiple_of(core * 8, 8), 8)
    kz_out = lambda i: remote(
        khalf.at[mine], kz.at[p // 2], kz_s.at[i // 2], kz_r.at[p // 2], (row_peers[i], q)
    )
    for i in range(2, D, 2):
        kz_out(i).start()
    kz[p // 2] = khalf[mine, :]

    turn_in(1)
    for i in range(2, D, 2):
        t = row_peers[i] // 2
        remote(
            khalf.at[mine], kz.at[t], kz_s.at[i // 2], kz_r.at[t], (row_peers[i], q)
        ).wait_recv()
    total = kz[0]
    for i in range(1, D // 2):
        total = total + kz[i]
    here = pl.ds(pl.multiple_of(q * SLICE + core * 8, 8), 8)
    there = pl.ds(pl.multiple_of(q * SLICE + 8 - core * 8, 8), 8)
    k_ref[here, :] = total
    half_out = remote(k_ref.at[here], k_ref.at[here], half_s, half_r, (other, q))
    half_out.start()
    remote(k_ref.at[there], k_ref.at[there], half_s, half_r, (other, q)).wait_recv()
    gather_col_start(k_ref, slab, k_s, k_r, p, q)
    for number in range(4):
        tile = lax.rem(q // 4 + number, 4)
        for i in range(4):
            t = 4 * tile + lax.rem(q + i, 4)

            @pl.when(t != q)
            def _():
                for at, (send, recv) in zip(HALVES, cp_sems):
                    remote(
                        cp_ref.at[at(t)], cp_ref.at[at(t)], send.at[0], recv.at[t], (p, t)
                    ).wait_recv()

        subtract(a_vm, cp_ref, local.turned_vq, tile_rows(tile))
        for at, sems in zip(HALVES, cq_sems):
            gather_row_pass(cq_ref, *sems, p, q, number, at=at)
    if panel == PANELS - 1:
        pltpu.make_async_copy(a_vm, local.a_out, local.store).start()
    gather_col_wait(k_ref, slab, k_s, k_r, p, q)
    middle = mid_ref[...]
    shift = dot3(dot3(middle, k_ref[...], 1, 0), middle, 1, 0)
    shift = split(0.5 * (shift + shift.T))
    for at, sems in zip(HALVES, cq_sems):
        gather_row_wait(cq_ref, *sems, p, q, at=at)
    for tile in range(4):
        rows = slice(tile * B, tile * B + B)
        rest = cq_ref[rows, :] - dot_split(split(vq_ref[rows, :]), shift, 1, 0)
        local.last[0][:, rows], local.last[1][:, rows] = split(rest.T)
    if panel < PANELS - 1:
        subtract(a_vm, vr_ref, local.last, slice(0, B))

    def drain():
        for h in range(2):
            gather_row_drain(cq_ref, *cq_sems[h], p, q, at=HALVES[h])
            gather_col_drain(cp_ref, HALVES[h], *cp_sems[h], p, q)
        gather_row_drain(pq_ref, pq_s, pq_r, p, q)
        for ref, at, send, recv in (
            (k_ref, slab, k_s, k_r), (pr_ref, piece, pr_s, pr_r),
            (g_ref, whole, g_s, g_r), (t_ref, whole, t_s, t_r),
        ):
            gather_col_drain(ref, at, send, recv, p, q)

        @pl.when(p != q)
        def _():
            turn_out(0).wait_send()
            turn_out(1).wait_send()

        pair_out.wait_send()
        half_out.wait_send()
        for i in range(2, D, 2):
            kz_out(i).wait_send()
        for i in range(1, D):
            kp_out(i).wait_send()
            x_out(col_peers[i], 0).wait_send()
            x_out(col_peers[i], 1).wait_send()

        @pl.when(row_owner)
        def _():
            for i in range(1, D):
                gram_out(i).wait_send()
                pq_out(i).wait_send()
                g_down(i).wait_send()
                t_down(i).wait_send()

            @pl.when(top_col)
            def _():
                for i in range(1, D):
                    block_out(i).wait_send()

        @pl.when(col_owner)
        def _():
            for i in range(1, D):
                pr_out(i).wait_send()

    return drain


def reduce_panels(matrix):
    vmem, anywhere = pl.BlockSpec(memory_space=pltpu.VMEM), pl.BlockSpec(memory_space=pl.ANY)
    buffers = lambda shapes: [pltpu.VMEM(shape, jnp.float32) for shape in shapes.values()]
    many, one = pltpu.SemaphoreType.DMA((D,)), pltpu.SemaphoreType.DMA
    right = jax.ShapeDtypeStruct((B, 4 * B), jnp.bfloat16)
    panel_set = buffers(PANEL_BUFFERS) + [many] * len(PANEL_MANY) + [one] * len(PANEL_ONE)
    return pl.pallas_call(
        reduce_kernel,
        out_shape=(
            jax.ShapeDtypeStruct((4 * B, 4 * B), jnp.float32),
            jax.ShapeDtypeStruct(TALL, jnp.float32), right, right,
        ),
        in_specs=[anywhere],
        out_specs=(anywhere, vmem, vmem, vmem),
        scratch_shapes=buffers(LOCAL_BUFFERS)
        + [pltpu.VMEM((B, 4 * B), jnp.bfloat16)] * 2
        + [pltpu.SemaphoreType.DMA((2,)), one]
        + panel_set * PANELS,
        compiler_params=pltpu.CompilerParams(
            collective_id=1, has_side_effects=True, vmem_limit_bytes=VMEM_LIMIT
        ),
        name="reduce_panels",
    )(matrix)


def finish_kernel(a_ref, vr_ref, high_ref, low_ref, out_ref):
    out_ref[...] = a_ref[...] - dot_split(
        split(vr_ref[...]), (high_ref[...], low_ref[...]), 1, 0
    )


def finish(matrix, vr, high, low):
    rows, size = B, 4 * B
    tile = lambda width: pl.BlockSpec((rows, width), lambda i: (i, 0))
    whole = pl.BlockSpec((B, size), lambda i: (0, 0))
    return pl.pallas_call(
        finish_kernel,
        out_shape=jax.ShapeDtypeStruct((size, size), jnp.float32),
        grid=(size // rows,),
        in_specs=[tile(size), tile(B), whole, whole],
        out_specs=tile(size),
        compiler_params=pltpu.CompilerParams(vmem_limit_bytes=VMEM_LIMIT),
        name="finish",
    )(matrix, vr, high, low)


def body(affinity):
    return finish(*reduce_panels(affinity))


def solution(mesh):
    return jax.shard_map(
        body,
        mesh=mesh,
        in_specs=(P("row", "col"),),
        out_specs=P("row", "col"),
        check_vma=False,
    )
```
